512 devices in a mesh: row: 16 (over z, core), col: 32 (over y, x).
Axes of the slice: x: 4, y: 8, z: 8, core: 2. Of those that a mesh axis runs over, the one named last changes fastest.
Arguments:
- grad: float32 [2048, 53248], P('row', 'col'), may hold values from -15 to 15
- momentum: float32 [2048, 53248], P('row', 'col'), may hold values from -6 to 6
- factor: float32 [53248, 256], P(('col', 'row')), may hold values from -0.02734375 to 0.02734375
Outputs:
- update: float32 [2048, 53248], P('row', 'col')
- momentum_out: float32 [2048, 53248], P('row', 'col')
- factor_out: float32 [53248, 256], P(('col', 'row'))
The draws below stay inside these ranges and needn't reach their ends.
All inputs are finite; a program needn't handle non-finite values.
Results may differ from the reference program's by a relative error of at most 0.000098.
Values sent between devices are 32-bit elements; how exact they have to be, the bound alone decides.
A program may use at most 64 MiB of HBM per device.

```python
import math
import jax
import jax.numpy as jnp
from jax import lax

COLS = 53248
RANK = 256
ROWS = 2048


def draw_grad(key, part):
    key = jax.random.fold_in(key, 11)
    keys = jax.random.split(key, 3)
    row_scales = jnp.exp(jax.random.uniform(keys[1], (ROWS, 1), jnp.float32) * jnp.log(10.0))
    col_scales = jnp.exp(jax.random.uniform(keys[2], (1, COLS), jnp.float32) * jnp.log(10.0))
    base_values = jnp.clip(jax.random.normal(keys[0], (ROWS, COLS), jnp.float32), -4.0, 4.0)
    return base_values * row_scales * col_scales * 0.03


def levels(own_key, shape, cuts, least, top_value):
    gain, own = 1.0, jax.random.fold_in(own_key, 6)
    for position, blocks in cuts:
        heights = jnp.exp(jax.random.uniform(jax.random.fold_in(own, position), (blocks,), jnp.float32, least / len(cuts), top_value / len(cuts)))
        gain = gain * jnp.repeat(heights, shape[position] // blocks).reshape([-1 if axis == position else 1 for axis in range(len(shape))])
    return gain


def bell_draw(own_key, extent, deviation, reach, shards=(), dtype=jnp.bfloat16):
    result = jax.random.normal(own_key, extent, jnp.float32) * deviation
    if len(shards) > 0:
        result = levels(own_key, extent, shards, -0.22, 0.18) * result
    return jnp.clip(result, min=-reach, max=reach).astype(dtype)


def setup_inputs(seed: int = 0) -> dict:
    key_of = jax.random.split(jax.random.key(seed), 4)
    grad = draw_grad(jax.random.fold_in(key_of[3], 71), 0)
    momentum = bell_draw(key_of[1], (ROWS, COLS), 1.0, 6.0, ((0, 16), (1, 32)), jnp.float32)
    factor = bell_draw(key_of[2], (COLS, RANK), COLS ** -0.5, 0.02734375, ((0, 512),), jnp.float32)
    return {"grad": grad, "momentum": momentum, "factor": factor}


feedback = 0.05
epsilon = 1e-06

def reference(grad, momentum, factor):
    highest = lax.Precision.HIGHEST
    summed = momentum + grad
    left = jnp.dot(summed.astype(jnp.float32), factor.astype(jnp.float32), precision=highest, preferred_element_type=jnp.float32)
    gram_matrix = jnp.dot(left.T.astype(jnp.float32), left.astype(jnp.float32), precision=highest, preferred_element_type=jnp.float32)
    lower_factor = jnp.linalg.cholesky(gram_matrix)
    left_basis = jax.scipy.linalg.solve_triangular(lower_factor, left.T, lower=True).T
    right_factor = lax.dot_general(summed.astype(jnp.float32), left_basis.astype(jnp.float32), (((0,), (0,)), ((), ())), precision=highest, preferred_element_type=jnp.float32)
    momentum_out = summed - feedback * jnp.dot(left_basis.astype(jnp.float32), right_factor.T.astype(jnp.float32), precision=highest, preferred_element_type=jnp.float32)
    square_sums = lax.optimization_barrier(jnp.sum(right_factor * right_factor, axis=0))
    factor_out = right_factor / (jnp.sqrt(square_sums) + epsilon)
    multiplier = math.sqrt(ROWS * COLS / RANK)
    update = multiplier * jnp.dot(left_basis.astype(jnp.float32), factor_out.T.astype(jnp.float32), precision=highest, preferred_element_type=jnp.float32)
    return (update, momentum_out, factor_out)
```

```python
import functools
import math

import jax
import jax.numpy as jnp
from jax import lax
from jax.experimental import pallas as pl
from jax.experimental.pallas import tpu as pltpu
from jax.sharding import PartitionSpec as P

feedback = 0.05
epsilon = 1e-06
MESH = pl.DeviceIdType.MESH
HIGHEST = lax.Precision.HIGHEST
F32 = jnp.float32

RANK = 256
HALF = 128
ZN = 8
RN = 16
CN = 32
ROWS = 128
COLS = 1664
OWN = COLS // RN
CHIP = 2 * OWN
SUBS = ((0, 32), (32, 24), (56, 24), (80, 24))
NS = len(SUBS)
CUT = 2
PANEL = 32


def dot(a, b):
    return jnp.dot(a, b, precision=HIGHEST, preferred_element_type=F32)


def dot_t(a, b):
    return lax.dot_general(
        a, b, (((1,), (1,)), ((), ())), precision=HIGHEST, preferred_element_type=F32
    )


def across_rows(x, t):
    return jnp.broadcast_to(x[t : t + 1, :], (8, 128))


def across_lanes(x, t):
    return jnp.broadcast_to(x[:, t : t + 1], (8, 128))


def reciprocal(p):
    r = pltpu.reciprocal(p, approx=True)
    return r * (2.0 - p * r)


def panel_step(k, m_ref, x_ref):
    groups = PANEL // 8
    row = lax.broadcasted_iota(jnp.int32, (8, 128), 0)
    m_halves = [h for h in (0, 1) if 128 * (h + 1) > k]
    x_halves = [h for h in (0, 1) if 128 * h < k + PANEL]
    rows = []
    for g in range(groups):
        at = slice(k + 8 * g, k + 8 * g + 8)
        held = {}
        for h in m_halves:
            held["m", h] = m_ref[h, at, :]
        for h in x_halves:
            held["x", h] = x_ref[h, at, :]
        rows.append(held)
    for s in range(groups):
        base = k + 8 * s
        half, lane = ("m", base // 128), base % 128
        column = [
            [across_lanes(rows[g][half], lane + t) for t in range(8)] if g >= s else None
            for g in range(groups)
        ]
        pivots = jnp.zeros((8, 128), F32)
        for t in range(8):
            pivot = across_rows(column[s][t], t)
            inverse = reciprocal(pivot)
            pivots = jnp.where(row == t, pivot, pivots)
            pivot_row = {h: across_rows(v, t) for h, v in rows[s].items()}
            entry = [across_rows(column[s][j], t) if j > t else None for j in range(8)]
            for g in range(s, groups):
                factor = column[g][t] * inverse
                if g == s:
                    factor = jnp.where(row > t, factor, 0.0)
                for j in range(t + 1, 8):
                    column[g][j] = column[g][j] - factor * entry[j]
                for h in rows[g]:
                    rows[g][h] = rows[g][h] - factor * pivot_row[h]
        scale = lax.rsqrt(pivots)
        scale = scale * (1.5 - 0.5 * pivots * scale * scale)
        for h in rows[s]:
            rows[s][h] = rows[s][h] * scale
    for g in range(groups):
        at = slice(k + 8 * g, k + 8 * g + 8)
        for (name, h), v in rows[g].items():
            (m_ref if name == "m" else x_ref)[h, at, :] = v


def trailing_step(k, m_ref, x_ref):
    end = k + PANEL
    if end >= RANK:
        return
    m_halves = [h for h in (0, 1) if 128 * (h + 1) > end]
    x_halves = [h for h in (0, 1) if 128 * h < end]
    scaled = jnp.concatenate([m_ref[h, k:end, :] for h in m_halves], axis=1)
    first = 128 * m_halves[0]
    scaled_t = jnp.transpose(scaled)
    other = jnp.concatenate([x_ref[h, k:end, :] for h in x_halves], axis=1)
    for a, b in ((end, end + PANEL), (end + PANEL, RANK)):
        if a >= b:
            continue
        left = scaled_t[a - first : b - first, :]
        change = dot(left, scaled)
        for n, h in enumerate(m_halves):
            m_ref[h, a:b, :] = m_ref[h, a:b, :] - change[:, 128 * n : 128 * n + 128]
        change = dot(left, other)
        for n, h in enumerate(x_halves):
            x_ref[h, a:b, :] = x_ref[h, a:b, :] - change[:, 128 * n : 128 * n + 128]


def kernel(
    grad_ref, momentum_ref, factor_ref, update_ref, out_ref, new_factor_ref,
    grad_v, summed, blocks, blocks_t, gathered, part_tiles, part_in, left_tiles, left_t,
    gram_part, gram_in, m_ref, x_ref, product, product_in, passing, right_p, right_f,
    square_part, square_in,
    load_sem, ring_send, ring_recv, pair_send, pair_recv,
    rs_send, rs_recv, half_send, half_recv, ring2_send, ring2_recv, pair2_send, pair2_recv,
    plane_send, plane_recv, line_send, line_recv, sister_send, sister_recv,
):
    r = lax.axis_index("row")
    c = lax.axis_index("col")
    z = r // 2
    core = lax.rem(r, 2)
    sister = (z * 2 + 1 - core, c)

    def ring(d):
        return lax.rem(z + d + 2 * ZN, ZN)

    toward = ((ring(1) * 2 + core, c), (ring(-1) * 2 + core, c))

    loads = [
        pltpu.make_async_copy(grad_ref, grad_v, load_sem.at[0]),
        pltpu.make_async_copy(momentum_ref, summed, load_sem.at[1]),
    ]
    for load in loads:
        load.start()

    barrier = pltpu.get_barrier_semaphore()

    def greet_line(d, _):
        pl.semaphore_signal(barrier, 1, device_id=(lax.rem(r + d, RN), c), device_id_type=MESH)
        return 0

    def greet_plane(d, _):
        pl.semaphore_signal(barrier, 1, device_id=(r, lax.rem(c + d, CN)), device_id_type=MESH)
        return 0

    lax.fori_loop(1, RN, greet_line, 0)
    lax.fori_loop(1, CN, greet_plane, 0)
    pl.semaphore_wait(barrier, RN - 1 + CN - 1)

    def at(zz, k, lo=0, n=OWN):
        return pl.ds(pl.multiple_of(zz * CHIP + k * OWN + lo, 8), n)

    def ring_gather(buf, sends, recvs, psend, precv):
        def pieces(way, step):
            if step < 4:
                return range(NS)
            return range(CUT) if way == 0 else range(CUT, NS)

        def hop(way, step, s):
            lo, n = SUBS[s]
            zz = ring(-(step - 1)) if way == 0 else ring(step - 1)
            ref = buf.at[at(zz, core, lo, n), :]
            return pltpu.make_async_remote_copy(
                src_ref=ref, dst_ref=ref,
                send_sem=sends.at[way, step - 1, s], recv_sem=recvs.at[way, step - 1, s],
                device_id=toward[way], device_id_type=MESH,
            )

        def over(way, step):
            if step < 4:
                lo, n = 0, OWN
            elif way == 0:
                lo, n = 0, SUBS[CUT][0]
            else:
                lo, n = SUBS[CUT][0], OWN - SUBS[CUT][0]
            zz = ring(-step) if way == 0 else ring(step)
            ref = buf.at[at(zz, core, lo, n), :]
            return pltpu.make_async_remote_copy(
                src_ref=ref, dst_ref=ref,
                send_sem=psend.at[way, step], recv_sem=precv.at[way, step],
                device_id=sister, device_id_type=MESH,
            )

        def start():
            for s in range(NS):
                for way in (0, 1):
                    hop(way, 1, s).start()
            over(0, 0).start()

        def take(step):
            for s in range(NS):
                for way in (0, 1):
                    if s in pieces(way, step):
                        hop(way, step, s).wait_recv()
                        if step < 4 and s in pieces(way, step + 1):
                            hop(way, step + 1, s).start()
            for way in (0, 1):
                over(way, step).start()

        def have(step):
            for way in (0, 1):
                if step > 0 or way == 0:
                    over(way, step).wait_recv()

        def finish():
            for step in range(1, 5):
                for way in (0, 1):
                    for s in pieces(way, step):
                        hop(way, step, s).wait_send()
            over(0, 0).wait_send()
            for step in range(1, 5):
                for way in (0, 1):
                    over(way, step).wait_send()

        return start, take, have, finish

    gathered[at(z, core), :] = factor_ref[...]
    start, take, have, finish = ring_gather(gathered, ring_send, ring_recv, pair_send, pair_recv)
    start()
    for load in loads:
        load.wait()
    for n in range(0, COLS, 128):
        lanes = slice(n, n + 128)
        summed[:, lanes] = summed[:, lanes] + grad_v[:, lanes]
    for b in range(ZN):
        block = summed[:, b * CHIP : (b + 1) * CHIP]
        blocks[b, :, 0:CHIP] = block
    for b in range(ZN):
        blocks_t[b] = jnp.transpose(blocks[b, :, 0:CHIP])

    def partial(zz):
        return dot(blocks[zz, :, 0:CHIP], gathered[pl.ds(pl.multiple_of(zz * CHIP, 8), CHIP), :])

    have(0)
    total = partial(z)
    for step in range(1, 5):
        take(step)
        if step > 1:
            have(step - 1)
            total = total + partial(ring(-(step - 1))) + partial(ring(step - 1))
    have(4)
    total = total + partial(ring(4))
    finish()

    for h in range(2):
        part_tiles[h] = total[:, 128 * h : 128 * h + 128]

    def tile(ref, q):
        return ref.at[q // 16, pl.ds(pl.multiple_of(lax.rem(q, 16) * 8, 8), 8), :]

    def spread(src, dst, index):
        def send(d, _):
            q = lax.rem(c + d, CN)
            pltpu.make_async_remote_copy(
                src_ref=src(q), dst_ref=dst,
                send_sem=plane_send.at[index], recv_sem=plane_recv.at[index],
                device_id=(r, q), device_id_type=MESH,
            ).start()
            return 0

        lax.fori_loop(1, CN, send, 0)

    def plane_wait(sem):
        pltpu.make_async_copy(
            part_in.at[pl.ds(0, CN - 1)], part_in.at[pl.ds(0, CN - 1)], sem
        ).wait()

    part_in[c] = part_tiles[c // 16, pl.ds(pl.multiple_of(lax.rem(c, 16) * 8, 8), 8), :]
    spread(lambda q: tile(part_tiles, q), part_in.at[c], 0)
    plane_wait(plane_recv.at[0])
    own_tile = part_in[0]
    for q in range(1, CN):
        own_tile = own_tile + part_in[q]
    left_tiles[c // 16, pl.ds(pl.multiple_of(lax.rem(c, 16) * 8, 8), 8), :] = own_tile
    spread(lambda q: tile(left_tiles, c), tile(left_tiles, c), 1)
    plane_wait(plane_recv.at[1])
    left = jnp.concatenate([left_tiles[0], left_tiles[1]], axis=1)

    for h in range(2):
        left_t[128 * h : 128 * h + 128, :] = jnp.transpose(left_tiles[h])
    gram_rows = dot(left_t[pl.ds(pl.multiple_of(c * 8, 8), 8), :], left)
    for h in range(2):
        gram_part[h] = gram_rows[:, 128 * h : 128 * h + 128]
    gram_in[r] = gram_part[core]

    def send_line(d, _):
        q = lax.rem(r + d, RN)
        pltpu.make_async_remote_copy(
            src_ref=gram_part.at[lax.rem(q, 2)], dst_ref=gram_in.at[r],
            send_sem=line_send, recv_sem=line_recv,
            device_id=(q, c), device_id_type=MESH,
        ).start()
        return 0

    lax.fori_loop(1, RN, send_line, 0)

    def give(dist):
        zz = ring(dist)
        return pltpu.make_async_remote_copy(
            src_ref=product.at[at(zz, 1 - core), :], dst_ref=product_in.at[zz],
            send_sem=half_send.at[dist], recv_sem=half_recv.at[dist],
            device_id=sister, device_id_type=MESH,
        )

    order = (4, 3, 5, 2, 6, 1, 7, 0)
    for dist in order:
        zz = ring(dist)
        product[pl.ds(pl.multiple_of(zz * CHIP, 8), CHIP), :] = dot(blocks_t[zz], left)
        give(dist).start()

    def add_sister(dist):
        zz = ring(dist)
        give(dist).wait_recv()
        product[at(zz, core), :] = product[at(zz, core), :] + product_in[zz]

    def onward(way, dist, s):
        lo, n = SUBS[s]
        zz = ring(dist) if way == 0 else ring(-dist)
        return pltpu.make_async_remote_copy(
            src_ref=product.at[at(zz, core, lo, n), :],
            dst_ref=passing.at[way, dist - 1, pl.ds(lo, n), :],
            send_sem=rs_send.at[way, dist - 1, s], recv_sem=rs_recv.at[way, dist - 1, s],
            device_id=toward[way], device_id_type=MESH,
        )

    def sub_range(way, dist):
        if dist < 4:
            return range(NS)
        return range(CUT) if way == 0 else range(CUT, NS)

    def scatter_start():
        add_sister(4)
        for s in range(CUT):
            onward(0, 4, s).start()
            onward(1, 4, CUT + s).start()

    def scatter(dist):
        if dist > 0:
            add_sister(dist)
            add_sister(8 - dist)
        else:
            add_sister(0)
        for s in range(NS):
            lo, n = SUBS[s]
            for way in (0, 1):
                zz = ring(dist) if way == 0 else ring(-dist)
                if s in sub_range(way, dist + 1):
                    onward(way, dist + 1, s).wait_recv()
                    rows = at(zz, core, lo, n)
                    product[rows, :] = product[rows, :] + passing[way, dist, lo : lo + n, :]
                if dist > 0:
                    onward(way, dist, s).start()

    def scatter_finish():
        for dist in range(8):
            give(dist).wait_send()
        for dist in range(1, 5):
            for way in (0, 1):
                for s in sub_range(way, dist):
                    onward(way, dist, s).wait_send()

    scatter_start()

    def line_wait(sem):
        pltpu.make_async_copy(
            gram_in.at[pl.ds(0, RN - 1)], gram_in.at[pl.ds(0, RN - 1)], sem
        ).wait()

    line_wait(line_recv)
    gram_tile = gram_in[0]
    for q in range(1, RN):
        gram_tile = gram_tile + gram_in[q]
    gram_at = pl.ds(pl.multiple_of(c * 8, 8), 8)
    m_ref[core, gram_at, :] = gram_tile
    spread(lambda q: m_ref.at[core, gram_at, :], m_ref.at[core, gram_at, :], 2)
    scatter(3)
    plane_wait(plane_recv.at[2])
    to_sister = pltpu.make_async_remote_copy(
        src_ref=m_ref.at[core], dst_ref=m_ref.at[core],
        send_sem=sister_send, recv_sem=sister_recv,
        device_id=sister, device_id_type=MESH,
    )
    to_sister.start()
    row = lax.broadcasted_iota(jnp.int32, (RANK, HALF), 0)
    lane = lax.broadcasted_iota(jnp.int32, (RANK, HALF), 1)
    for h in range(2):
        x_ref[h] = jnp.where(row == lane + 128 * h, 1.0, 0.0).astype(F32)
    plane_wait(plane_send.at[2])
    to_sister.wait()

    start2, take2, have2, finish2 = ring_gather(
        right_p, ring2_send, ring2_recv, pair2_send, pair2_recv
    )

    def own_block():
        scatter(0)
        right_p[at(z, core), :] = product[at(z, core), :]
        start2()

    beside = [
        lambda: scatter(2),
        lambda: scatter(1),
        own_block,
        lambda: take2(1),
        lambda: take2(2),
        lambda: take2(3),
        lambda: take2(4),
    ]
    for n, k in enumerate(range(0, RANK, PANEL)):
        panel_step(k, m_ref, x_ref)
        trailing_step(k, m_ref, x_ref)
        if n < len(beside):
            beside[n]()
    for step in range(5):
        have2(step)

    inverse = jnp.concatenate([x_ref[0], x_ref[1]], axis=1)
    basis = dot_t(left, inverse)

    def right_rows(n, squares):
        rows = pl.ds(pl.multiple_of(n * 128, 128), 128)
        value = dot_t(right_p[rows, :], inverse)
        right_f[rows, :] = value
        square = value * value
        return squares + jnp.sum(square.reshape(16, 8, RANK), axis=0)

    squares = lax.fori_loop(0, COLS // 128, right_rows, jnp.zeros((8, RANK), F32))
    squares = jnp.sum(squares, axis=0, keepdims=True)
    which = lax.broadcasted_iota(jnp.int32, (8, HALF), 0)
    square_tile = jnp.where(which == 0, squares[:, 0:128], squares[:, 128:256])
    square_part[...] = square_tile
    square_in[c] = square_tile
    spread(lambda q: square_part, square_in.at[c], 3)

    for n in range(0, COLS, 128):
        lanes = slice(n, n + 128)
        out_ref[:, lanes] = summed[:, lanes] - feedback * dot_t(basis, right_f[n : n + 128, :])

    plane_wait(plane_recv.at[3])
    square_sum = square_in[0]
    for q in range(1, CN):
        square_sum = square_sum + square_in[q]
    norm = jnp.sqrt(square_sum) + epsilon
    norm = jnp.concatenate([norm[0:1, :], norm[1:2, :]], axis=1)
    new_factor_ref[...] = right_f[at(z, core), :] / norm
    multiplier = math.sqrt(ROWS * RN * COLS * CN / RANK)
    scaled_basis = basis * (multiplier / norm)
    for n in range(0, COLS, 128):
        lanes = slice(n, n + 128)
        update_ref[:, lanes] = dot_t(scaled_basis, right_f[n : n + 128, :])

    for index in (0, 1, 3):
        plane_wait(plane_send.at[index])
    line_wait(line_send)
    scatter_finish()
    finish2()


def per_device(grad, momentum, factor):
    vmem = pl.BlockSpec(memory_space=pltpu.VMEM)
    hbm = pl.BlockSpec(memory_space=pl.ANY)
    dma = pltpu.SemaphoreType.DMA
    out_shape = (
        jax.ShapeDtypeStruct((ROWS, COLS), F32),
        jax.ShapeDtypeStruct((ROWS, COLS), F32),
        jax.ShapeDtypeStruct((OWN, RANK), F32),
    )
    scratch = [
        pltpu.VMEM((ROWS, COLS), F32),
        pltpu.VMEM((ROWS, COLS), F32),
        pltpu.VMEM((ZN, ROWS, 256), F32),
        pltpu.VMEM((ZN, CHIP, ROWS), F32),
        pltpu.VMEM((COLS, RANK), F32),
        pltpu.VMEM((2, ROWS, HALF), F32),
        pltpu.VMEM((CN, 8, HALF), F32),
        pltpu.VMEM((2, ROWS, HALF), F32),
        pltpu.VMEM((RANK, ROWS), F32),
        pltpu.VMEM((2, 8, HALF), F32),
        pltpu.VMEM((RN, 8, HALF), F32),
        pltpu.VMEM((2, RANK, HALF), F32),
        pltpu.VMEM((2, RANK, HALF), F32),
        pltpu.VMEM((COLS, RANK), F32),
        pltpu.VMEM((ZN, OWN, RANK), F32),
        pltpu.VMEM((2, 4, OWN, RANK), F32),
        pltpu.VMEM((COLS, RANK), F32),
        pltpu.VMEM((COLS, RANK), F32),
        pltpu.VMEM((8, HALF), F32),
        pltpu.VMEM((CN, 8, HALF), F32),
        dma((2,)),
        dma((2, 4, NS)), dma((2, 4, NS)),
        dma((2, 5)), dma((2, 5)),
        dma((2, 4, NS)), dma((2, 4, NS)),
        dma((8,)), dma((8,)),
        dma((2, 4, NS)), dma((2, 4, NS)),
        dma((2, 5)), dma((2, 5)),
        dma((4,)), dma((4,)),
        dma, dma,
        dma, dma,
    ]
    return pl.pallas_call(
        kernel,
        out_shape=out_shape,
        in_specs=[hbm, hbm, vmem],
        out_specs=(vmem, vmem, vmem),
        scratch_shapes=scratch,
        compiler_params=pltpu.CompilerParams(
            collective_id=0, has_side_effects=True, vmem_limit_bytes=48 * 1024 * 1024
        ),
    )(grad, momentum, factor)


def solution(mesh):
    return jax.shard_map(
        per_device,
        mesh=mesh,
        in_specs=(P("row", "col"), P("row", "col"), P(("col", "row"), None)),
        out_specs=(P("row", "col"), P("row", "col"), P(("col", "row"), None)),
        check_vma=False,
    )
```

```python
import functools
import math

import jax
import jax.numpy as jnp
from jax import lax
from jax.experimental import pallas as pl
from jax.experimental.pallas import tpu as pltpu
from jax.sharding import PartitionSpec as P

feedback = 0.05
epsilon = 1e-06
MESH = pl.DeviceIdType.MESH
HIGHEST = lax.Precision.HIGHEST
F32 = jnp.float32
BF16 = jnp.bfloat16

RANK = 256
HALF = 128
ZN = 8
RN = 16
CN = 32
ROWS = 128
COLS = 1664
OWN = COLS // RN
CHIP = 2 * OWN
SUBS = ((0, 32), (32, 24), (56, 24), (80, 24))
NS = len(SUBS)
CUT = 2
PARENT = {1: 0, 2: 1, 3: 2, 4: 2}
SIGN = (1, -1)
LOADS = 4
PANEL = 32


def dot(a, b):
    return jnp.dot(a, b, precision=HIGHEST, preferred_element_type=F32)


def dot_t(a, b):
    return lax.dot_general(
        a, b, (((1,), (1,)), ((), ())), precision=HIGHEST, preferred_element_type=F32
    )


def split(a):
    high = a.astype(BF16)
    return high, (a - high.astype(F32)).astype(BF16)


def split_dot_t(a, b):
    def part(x, y):
        return lax.dot_general(x, y, (((1,), (1,)), ((), ())), preferred_element_type=F32)

    return part(a[0], b[0]) + (part(a[0], b[1]) + part(a[1], b[0]))


def across_rows(x, t):
    return jnp.broadcast_to(x[t : t + 1, :], (8, 128))


def across_lanes(x, t):
    return jnp.broadcast_to(x[:, t : t + 1], (8, 128))


def reciprocal(p):
    r = pltpu.reciprocal(p, approx=True)
    return r * (2.0 - p * r)


def panel_step(k, m_ref, x_ref):
    groups = PANEL // 8
    row = lax.broadcasted_iota(jnp.int32, (8, 128), 0)
    m_halves = [h for h in (0, 1) if 128 * (h + 1) > k]
    x_halves = [h for h in (0, 1) if 128 * h < k + PANEL]
    rows = []
    for g in range(groups):
        at = slice(k + 8 * g, k + 8 * g + 8)
        held = {}
        for h in m_halves:
            held["m", h] = m_ref[h, at, :]
        for h in x_halves:
            held["x", h] = x_ref[h, at, :]
        rows.append(held)
    for s in range(groups):
        base = k + 8 * s
        half, lane = ("m", base // 128), base % 128
        column = [
            [across_lanes(rows[g][half], lane + t) for t in range(8)] if g >= s else None
            for g in range(groups)
        ]
        pivots = jnp.zeros((8, 128), F32)
        for t in range(8):
            pivot = across_rows(column[s][t], t)
            inverse = reciprocal(pivot)
            pivots = jnp.where(row == t, pivot, pivots)
            pivot_row = {h: across_rows(v, t) for h, v in rows[s].items()}
            entry = [across_rows(column[s][j], t) if j > t else None for j in range(8)]
            for g in range(s, groups):
                factor = column[g][t] * inverse
                if g == s:
                    factor = jnp.where(row > t, factor, 0.0)
                for j in range(t + 1, 8):
                    column[g][j] = column[g][j] - factor * entry[j]
                for h in rows[g]:
                    rows[g][h] = rows[g][h] - factor * pivot_row[h]
        scale = lax.rsqrt(pivots)
        scale = scale * (1.5 - 0.5 * pivots * scale * scale)
        for h in rows[s]:
            rows[s][h] = rows[s][h] * scale
    for g in range(groups):
        at = slice(k + 8 * g, k + 8 * g + 8)
        for (name, h), v in rows[g].items():
            (m_ref if name == "m" else x_ref)[h, at, :] = v


def trailing_step(k, m_ref, x_ref):
    end = k + PANEL
    if end >= RANK:
        return
    m_halves = [h for h in (0, 1) if 128 * (h + 1) > end]
    x_halves = [h for h in (0, 1) if 128 * h < end]
    scaled = jnp.concatenate([m_ref[h, k:end, :] for h in m_halves], axis=1)
    first = 128 * m_halves[0]
    scaled_t = jnp.transpose(scaled)
    other = jnp.concatenate([x_ref[h, k:end, :] for h in x_halves], axis=1)
    for a, b in ((end, end + PANEL), (end + PANEL, RANK)):
        if a >= b:
            continue
        left = scaled_t[a - first : b - first, :]
        change = dot(left, scaled)
        for n, h in enumerate(m_halves):
            m_ref[h, a:b, :] = m_ref[h, a:b, :] - change[:, 128 * n : 128 * n + 128]
        change = dot(left, other)
        for n, h in enumerate(x_halves):
            x_ref[h, a:b, :] = x_ref[h, a:b, :] - change[:, 128 * n : 128 * n + 128]


def kernel(
    grad_ref, momentum_ref, factor_ref,
    out_ref, new_factor_ref, basis_ref, right_high, right_low,
    grad_v, summed, blocks, blocks_t, gathered, part_tiles, part_in, left_tiles, left_t,
    gram_part, gram_in, m_ref, x_ref, product, product_in, passing, right_p, own_right,
    square_part, square_in,
    load_sem, ring_send, ring_recv, pair_send, pair_recv,
    rs_send, rs_recv, half_send, half_recv, ring2_send, ring2_recv, pair2_send, pair2_recv,
    plane_send, plane_recv, line_send, line_recv, sister_send, sister_recv,
):
    r = lax.axis_index("row")
    c = lax.axis_index("col")
    z = r // 2
    core = lax.rem(r, 2)
    y = c // 4
    x = lax.rem(c, 4)
    sister = (z * 2 + 1 - core, c)

    def ring(d):
        return lax.rem(z + d + 2 * ZN, ZN)

    def along(d):
        return (ring(d) * 2 + core, c)

    def at(zz, k, lo=0, n=OWN):
        return pl.ds(pl.multiple_of(zz * CHIP + k * OWN + lo, 8), n)

    own_load = pltpu.make_async_copy(
        factor_ref, gathered.at[at(z, core), :], load_sem.at[2 * LOADS]
    )
    own_load.start()
    loads = []
    for n in range(LOADS):
        rows = pl.ds(n * (ROWS // LOADS), ROWS // LOADS)
        for m, (src, dst) in enumerate(((grad_ref, grad_v), (momentum_ref, summed))):
            loads.append(
                pltpu.make_async_copy(src.at[rows, :], dst.at[rows, :], load_sem.at[2 * n + m])
            )
    for load in loads:
        load.start()

    barrier = pltpu.get_barrier_semaphore()

    def greet_line(d, _):
        pl.semaphore_signal(barrier, 1, device_id=(lax.rem(r + d, RN), c), device_id_type=MESH)
        return 0

    def greet_plane(d, _):
        pl.semaphore_signal(barrier, 1, device_id=(r, lax.rem(c + d, CN)), device_id_type=MESH)
        return 0

    lax.fori_loop(1, RN, greet_line, 0)
    lax.fori_loop(1, CN, greet_plane, 0)
    own_load.wait()
    pl.semaphore_wait(barrier, RN - 1 + CN - 1)

    def pieces(dist, way):
        if dist < 4:
            return range(NS)
        return range(CUT) if way == 0 else range(CUT, NS)

    def ring_gather(buf, sends, recvs, psend, precv):
        def hop(way, dist, s):
            lo, n = SUBS[s]
            ref = buf.at[at(ring(-SIGN[way] * PARENT[dist]), core, lo, n), :]
            return pltpu.make_async_remote_copy(
                src_ref=ref, dst_ref=ref,
                send_sem=sends.at[way, dist - 1, s], recv_sem=recvs.at[way, dist - 1, s],
                device_id=along(SIGN[way] * (dist - PARENT[dist])), device_id_type=MESH,
            )

        def over(way, dist):
            if dist < 4:
                lo, n = 0, OWN
            elif way == 0:
                lo, n = 0, SUBS[CUT][0]
            else:
                lo, n = SUBS[CUT][0], OWN - SUBS[CUT][0]
            ref = buf.at[at(ring(-SIGN[way] * dist), core, lo, n), :]
            return pltpu.make_async_remote_copy(
                src_ref=ref, dst_ref=ref,
                send_sem=psend.at[way, dist], recv_sem=precv.at[way, dist],
                device_id=sister, device_id_type=MESH,
            )

        def start(s):
            for way in (0, 1):
                hop(way, 1, s).start()

        def take(dist):
            for s in range(NS):
                for way in (0, 1):
                    if s not in pieces(dist, way):
                        continue
                    hop(way, dist, s).wait_recv()
                    for later in (4, 3, 2):
                        if PARENT[later] == dist and s in pieces(later, way):
                            hop(way, later, s).start()
            for way in (0, 1):
                over(way, dist).start()

        def have(dist):
            for way in (0, 1):
                if dist > 0 or way == 0:
                    over(way, dist).wait_recv()

        def finish():
            over(0, 0).wait_send()
            for dist in range(1, 5):
                for way in (0, 1):
                    over(way, dist).wait_send()
                    for s in pieces(dist, way):
                        hop(way, dist, s).wait_send()

        return start, take, have, finish, over

    start, take, have, finish, over = ring_gather(
        gathered, ring_send, ring_recv, pair_send, pair_recv
    )
    for s in range(NS):
        start(s)
    over(0, 0).start()
    for load in loads:
        load.wait()
    for n in range(0, COLS, 128):
        lanes = slice(n, n + 128)
        summed[:, lanes] = summed[:, lanes] + grad_v[:, lanes]
    for b in range(ZN):
        blocks[b, :, 0:CHIP] = summed[:, b * CHIP : (b + 1) * CHIP]

    def partial(zz):
        return dot(blocks[zz, :, 0:CHIP], gathered[pl.ds(pl.multiple_of(zz * CHIP, 8), CHIP), :])

    take(1)
    have(0)
    total = partial(z)
    take(2)
    have(1)
    total = total + partial(ring(-1)) + partial(ring(1))
    take(3)
    take(4)
    have(2)
    total = total + partial(ring(-2)) + partial(ring(2))
    have(3)
    total = total + partial(ring(-3)) + partial(ring(3))
    have(4)
    total = total + partial(ring(4))

    for h in range(2):
        part_tiles[h] = total[:, 128 * h : 128 * h + 128]

    def tile(ref, q):
        return ref.at[q // 16, pl.ds(pl.multiple_of(lax.rem(q, 16) * 8, 8), 8), :]

    def farthest_first(n, middle):
        return middle + (1 - 2 * lax.rem(n, 2)) * ((n + 1) // 2)

    def spread(src, dst, index):
        def send(dy, dx):
            q = lax.rem(y + dy, 8) * 4 + lax.rem(x + dx, 4)
            pltpu.make_async_remote_copy(
                src_ref=src(q), dst_ref=dst,
                send_sem=plane_send.at[index], recv_sem=plane_recv.at[index],
                device_id=(r, q), device_id_type=MESH,
            ).start()

        def send_row(n, _):
            dy = farthest_first(n, 4)
            for dx in (2, 1, 3, 0):
                send(dy, dx)
            return 0

        lax.fori_loop(0, 7, send_row, 0)
        for dx in (2, 1, 3):
            send(0, dx)

    def plane_wait(sem):
        pltpu.make_async_copy(
            part_in.at[pl.ds(0, CN - 1)], part_in.at[pl.ds(0, CN - 1)], sem
        ).wait()

    spread(lambda q: tile(part_tiles, q), part_in.at[c], 0)
    part_in[c] = part_tiles[c // 16, pl.ds(pl.multiple_of(lax.rem(c, 16) * 8, 8), 8), :]
    for b in range(ZN):
        blocks_t[b] = jnp.transpose(blocks[b, :, 0:CHIP])
    finish()
    plane_wait(plane_recv.at[0])
    own_tile = part_in[0]
    for q in range(1, CN):
        own_tile = own_tile + part_in[q]
    left_tiles[c // 16, pl.ds(pl.multiple_of(lax.rem(c, 16) * 8, 8), 8), :] = own_tile
    spread(lambda q: tile(left_tiles, c), tile(left_tiles, c), 1)
    plane_wait(plane_recv.at[1])
    left = jnp.concatenate([left_tiles[0], left_tiles[1]], axis=1)

    for h in range(2):
        left_t[128 * h : 128 * h + 128, :] = jnp.transpose(left_tiles[h])
    gram_rows = dot(left_t[pl.ds(pl.multiple_of(c * 8, 8), 8), :], left)
    for h in range(2):
        gram_part[h] = gram_rows[:, 128 * h : 128 * h + 128]

    def send_line(q):
        pltpu.make_async_remote_copy(
            src_ref=gram_part.at[lax.rem(q, 2)], dst_ref=gram_in.at[r],
            send_sem=line_send, recv_sem=line_recv,
            device_id=(q, c), device_id_type=MESH,
        ).start()

    def send_chip(n, _):
        zz = ring(farthest_first(n, 4))
        for k in range(2):
            send_line(zz * 2 + k)
        return 0

    lax.fori_loop(0, 7, send_chip, 0)
    send_line(z * 2 + 1 - core)
    gram_in[r] = gram_part[core]

    def give(dist):
        zz = ring(dist)
        return pltpu.make_async_remote_copy(
            src_ref=product.at[at(zz, 1 - core), :], dst_ref=product_in.at[zz],
            send_sem=half_send.at[dist], recv_sem=half_recv.at[dist],
            device_id=sister, device_id_type=MESH,
        )

    def multiply(dist):
        zz = ring(dist)
        product[pl.ds(pl.multiple_of(zz * CHIP, 8), CHIP), :] = dot(blocks_t[zz], left)
        give(dist).start()

    def add_sister(dist):
        zz = ring(dist)
        give(dist).wait_recv()
        product[at(zz, core), :] = product[at(zz, core), :] + product_in[zz]

    def onward(way, dist, s):
        lo, n = SUBS[s]
        return pltpu.make_async_remote_copy(
            src_ref=product.at[at(ring(SIGN[way] * dist), core, lo, n), :],
            dst_ref=passing.at[way, dist - 1, pl.ds(lo, n), :],
            send_sem=rs_send.at[way, dist - 1, s], recv_sem=rs_recv.at[way, dist - 1, s],
            device_id=along(SIGN[way] * (dist - PARENT[dist])), device_id_type=MESH,
        )

    def scatter(dist, after):
        for s in range(NS):
            lo, n = SUBS[s]
            for way in (0, 1):
                rows = at(ring(SIGN[way] * dist), core, lo, n)
                value = product[rows, :]
                for earlier in (3, 4, 2, 1):
                    if PARENT[earlier] == dist and s in pieces(earlier, way):
                        onward(way, earlier, s).wait_recv()
                        value = value + passing[way, earlier - 1, lo : lo + n, :]
                product[rows, :] = value
                if dist > 0:
                    onward(way, dist, s).start()
            after(s)

    def scatter_finish():
        for dist in range(8):
            give(dist).wait_send()
        for dist in range(1, 5):
            for way in (0, 1):
                for s in pieces(dist, way):
                    onward(way, dist, s).wait_send()

    for dist in (4, 3, 5, 2, 6):
        multiply(dist)
    add_sister(4)
    for s in range(CUT):
        onward(0, 4, s).start()
        onward(1, 4, CUT + s).start()
    add_sister(3)
    add_sister(5)
    for s in range(NS):
        for way in (0, 1):
            onward(way, 3, s).start()
    for dist in (1, 7, 0):
        multiply(dist)
    for dist in (2, 6, 1, 7, 0):
        add_sister(dist)

    def line_wait(sem):
        pltpu.make_async_copy(
            gram_in.at[pl.ds(0, RN - 1)], gram_in.at[pl.ds(0, RN - 1)], sem
        ).wait()

    line_wait(line_recv)
    gram_tile = gram_in[0]
    for q in range(1, RN):
        gram_tile = gram_tile + gram_in[q]
    gram_at = pl.ds(pl.multiple_of(c * 8, 8), 8)
    m_ref[core, gram_at, :] = gram_tile
    spread(lambda q: m_ref.at[core, gram_at, :], m_ref.at[core, gram_at, :], 2)
    row = lax.broadcasted_iota(jnp.int32, (RANK, HALF), 0)
    lane = lax.broadcasted_iota(jnp.int32, (RANK, HALF), 1)
    for h in range(2):
        x_ref[h] = jnp.where(row == lane + 128 * h, 1.0, 0.0).astype(F32)

    def nothing(s):
        pass

    scatter(2, nothing)
    scatter(1, nothing)
    plane_wait(plane_recv.at[2])
    to_sister = pltpu.make_async_remote_copy(
        src_ref=m_ref.at[core], dst_ref=m_ref.at[core],
        send_sem=sister_send, recv_sem=sister_recv,
        device_id=sister, device_id_type=MESH,
    )
    to_sister.start()
    start2, take2, have2, finish2, over2 = ring_gather(
        right_p, ring2_send, ring2_recv, pair2_send, pair2_recv
    )

    def gather_piece(s):
        lo, n = SUBS[s]
        rows = at(z, core, lo, n)
        right_p[rows, :] = product[rows, :]
        start2(s)

    scatter(0, gather_piece)
    over2(0, 0).start()
    plane_wait(plane_send.at[2])
    to_sister.wait()

    beside = {1: (1,), 3: (2,), 6: (3, 4)}
    for n, k in enumerate(range(0, RANK, PANEL)):
        panel_step(k, m_ref, x_ref)
        trailing_step(k, m_ref, x_ref)
        for dist in beside.get(n, ()):
            take2(dist)

    inverse = jnp.concatenate([x_ref[0], x_ref[1]], axis=1)

    def right_block(zz, own=False):
        rows = pl.ds(pl.multiple_of(zz * CHIP, 16), CHIP)
        value = dot_t(right_p[rows, :], inverse)
        high, low = split(value)
        right_high[rows, :] = high
        right_low[rows, :] = low
        if own:
            own_right[...] = value
        return jnp.sum((value * value).reshape(CHIP // 8, 8, RANK), axis=0)

    squares = jnp.zeros((8, RANK), F32)
    basis = dot_t(left, inverse)
    for dist in range(5):
        have2(dist)
        if dist == 0:
            squares = squares + right_block(z, own=True)
        elif dist == 4:
            squares = squares + right_block(ring(4))
        else:
            squares = squares + right_block(ring(-dist)) + right_block(ring(dist))
    squares = jnp.sum(squares, axis=0, keepdims=True)
    which = lax.broadcasted_iota(jnp.int32, (8, HALF), 0)
    square_tile = jnp.where(which == 0, squares[:, 0:128], squares[:, 128:256])
    square_part[...] = square_tile
    square_in[c] = square_tile
    spread(lambda q: square_part, square_in.at[c], 3)

    basis_split = split(basis)
    for n in range(0, COLS, 128):
        lanes = slice(n, n + 128)
        right_n = (right_high[lanes, :], right_low[lanes, :])
        out_ref[:, lanes] = summed[:, lanes] - feedback * split_dot_t(basis_split, right_n)
    for index in (0, 1):
        plane_wait(plane_send.at[index])
    line_wait(line_send)
    scatter_finish()
    finish2()

    plane_wait(plane_recv.at[3])
    square_sum = square_in[0]
    for q in range(1, CN):
        square_sum = square_sum + square_in[q]
    norm = jnp.sqrt(square_sum) + epsilon
    norm = jnp.concatenate([norm[0:1, :], norm[1:2, :]], axis=1)
    mine = pl.ds(pl.multiple_of(core * OWN, 8), OWN)
    new_factor_ref[...] = own_right[mine, :] / norm
    multiplier = math.sqrt(ROWS * RN * COLS * CN / RANK)
    basis_ref[...] = basis * (multiplier / norm)
    plane_wait(plane_send.at[3])


def write_kernel(
    momentum_v, factor_v, basis_ref, right_high, right_low, update_ref, out_ref, new_factor_ref,
    update_v, sems,
):
    copies = [pltpu.make_async_copy(factor_v, new_factor_ref, sems.at[0])]
    step = ROWS // LOADS
    for n in range(LOADS):
        rows = pl.ds(n * step, step)
        copies.append(
            pltpu.make_async_copy(momentum_v.at[rows, :], out_ref.at[rows, :], sems.at[1 + n])
        )
    for copy in copies:
        copy.start()
    basis = split(basis_ref[...])
    for i, n in enumerate(range(0, COLS, 128)):
        lanes = slice(n, n + 128)
        update_v[:, lanes] = split_dot_t(basis, (right_high[lanes, :], right_low[lanes, :]))
        copy = pltpu.make_async_copy(
            update_v.at[:, pl.ds(n, 128)], update_ref.at[:, pl.ds(n, 128)], sems.at[1 + LOADS + i]
        )
        copy.start()
        copies.append(copy)
    for copy in copies:
        copy.wait()


def per_device(grad, momentum, factor):
    vmem = pl.BlockSpec(memory_space=pltpu.VMEM)
    hbm = pl.BlockSpec(memory_space=pltpu.HBM)
    dma = pltpu.SemaphoreType.DMA
    out_shape = (
        jax.ShapeDtypeStruct((ROWS, COLS), F32),
        jax.ShapeDtypeStruct((OWN, RANK), F32),
        jax.ShapeDtypeStruct((ROWS, RANK), F32),
        jax.ShapeDtypeStruct((COLS, RANK), BF16),
        jax.ShapeDtypeStruct((COLS, RANK), BF16),
    )
    scratch = [
        pltpu.VMEM((ROWS, COLS), F32),
        pltpu.VMEM((ROWS, COLS), F32),
        pltpu.VMEM((ZN, ROWS, 256), F32),
        pltpu.VMEM((ZN, CHIP, ROWS), F32),
        pltpu.VMEM((COLS, RANK), F32),
        pltpu.VMEM((2, ROWS, HALF), F32),
        pltpu.VMEM((CN, 8, HALF), F32),
        pltpu.VMEM((2, ROWS, HALF), F32),
        pltpu.VMEM((RANK, ROWS), F32),
        pltpu.VMEM((2, 8, HALF), F32),
        pltpu.VMEM((RN, 8, HALF), F32),
        pltpu.VMEM((2, RANK, HALF), F32),
        pltpu.VMEM((2, RANK, HALF), F32),
        pltpu.VMEM((COLS, RANK), F32),
        pltpu.VMEM((ZN, OWN, RANK), F32),
        pltpu.VMEM((2, 4, OWN, RANK), F32),
        pltpu.VMEM((COLS, RANK), F32),
        pltpu.VMEM((CHIP, RANK), F32),
        pltpu.VMEM((8, HALF), F32),
        pltpu.VMEM((CN, 8, HALF), F32),
        dma((2 * LOADS + 1,)),
        dma((2, 4, NS)), dma((2, 4, NS)),
        dma((2, 5)), dma((2, 5)),
        dma((2, 4, NS)), dma((2, 4, NS)),
        dma((8,)), dma((8,)),
        dma((2, 4, NS)), dma((2, 4, NS)),
        dma((2, 5)), dma((2, 5)),
        dma((4,)), dma((4,)),
        dma, dma,
        dma, dma,
    ]
    sent = pl.pallas_call(
        kernel,
        out_shape=out_shape,
        in_specs=[hbm, hbm, hbm],
        out_specs=(vmem,) * 5,
        scratch_shapes=scratch,
        compiler_params=pltpu.CompilerParams(
            collective_id=0, has_side_effects=True, vmem_limit_bytes=52224 * 1024
        ),
    )(grad, momentum, factor)
    full = jax.ShapeDtypeStruct((ROWS, COLS), F32)
    return pl.pallas_call(
        write_kernel,
        out_shape=(full, full, jax.ShapeDtypeStruct((OWN, RANK), F32)),
        in_specs=[vmem] * 5,
        out_specs=(hbm,) * 3,
        scratch_shapes=[pltpu.VMEM((ROWS, COLS), F32), dma((1 + LOADS + COLS // 128,))],
        compiler_params=pltpu.CompilerParams(vmem_limit_bytes=16 * 1024 * 1024),
    )(*sent)


def solution(mesh):
    return jax.shard_map(
        per_device,
        mesh=mesh,
        in_specs=(P("row", "col"), P("row", "col"), P(("col", "row"), None)),
        out_specs=(P("row", "col"), P("row", "col"), P(("col", "row"), None)),
        check_vma=False,
    )
```

```python
import functools
import math

import jax
import jax.numpy as jnp
from jax import lax
from jax.experimental import pallas as pl
from jax.experimental.pallas import tpu as pltpu
from jax.sharding import PartitionSpec as P

feedback = 0.05
epsilon = 1e-06
MESH = pl.DeviceIdType.MESH
HIGHEST = lax.Precision.HIGHEST
F32 = jnp.float32
BF16 = jnp.bfloat16

RANK = 256
HALF = 128
ZN = 8
RN = 16
CN = 32
ROWS = 128
COLS = 1664
OWN = COLS // RN
CHIP = 2 * OWN
SUBS = ((0, 32), (32, 24), (56, 24), (80, 24))
NS = len(SUBS)
CUT = 2
PARENT = {1: 0, 2: 1, 3: 2, 4: 2}
SIGN = (1, -1)
LOADS = 4
PANEL = 32


def dot(a, b):
    return jnp.dot(a, b, precision=HIGHEST, preferred_element_type=F32)


def dot_t(a, b):
    return lax.dot_general(
        a, b, (((1,), (1,)), ((), ())), precision=HIGHEST, preferred_element_type=F32
    )


def split(a):
    high = a.astype(BF16)
    return high, (a - high.astype(F32)).astype(BF16)


def split_dot_t(a, b):
    def part(x, y):
        return lax.dot_general(x, y, (((1,), (1,)), ((), ())), preferred_element_type=F32)

    return part(a[0], b[0]) + (part(a[0], b[1]) + part(a[1], b[0]))


def across_rows(x, t):
    return jnp.broadcast_to(x[t : t + 1, :], (8, 128))


def across_lanes(x, t):
    return jnp.broadcast_to(x[:, t : t + 1], (8, 128))


def reciprocal(p):
    r = pltpu.reciprocal(p, approx=True)
    return r * (2.0 - p * r)


def panel_step(k, m_ref, x_ref):
    groups = PANEL // 8
    row = lax.broadcasted_iota(jnp.int32, (8, 128), 0)
    m_halves = [h for h in (0, 1) if 128 * (h + 1) > k]
    x_halves = [h for h in (0, 1) if 128 * h < k + PANEL]
    rows = []
    for g in range(groups):
        at = slice(k + 8 * g, k + 8 * g + 8)
        held = {}
        for h in m_halves:
            held["m", h] = m_ref[h, at, :]
        for h in x_halves:
            held["x", h] = x_ref[h, at, :]
        rows.append(held)
    for s in range(groups):
        base = k + 8 * s
        half, lane = ("m", base // 128), base % 128
        column = [
            [across_lanes(rows[g][half], lane + t) for t in range(8)] if g >= s else None
            for g in range(groups)
        ]
        pivots = jnp.zeros((8, 128), F32)
        for t in range(8):
            pivot = across_rows(column[s][t], t)
            inverse = reciprocal(pivot)
            pivots = jnp.where(row == t, pivot, pivots)
            pivot_row = {h: across_rows(v, t) for h, v in rows[s].items()}
            entry = [across_rows(column[s][j], t) if j > t else None for j in range(8)]
            for g in range(s, groups):
                factor = column[g][t] * inverse
                if g == s:
                    factor = jnp.where(row > t, factor, 0.0)
                for j in range(t + 1, 8):
                    column[g][j] = column[g][j] - factor * entry[j]
                for h in rows[g]:
                    rows[g][h] = rows[g][h] - factor * pivot_row[h]
        scale = lax.rsqrt(pivots)
        scale = scale * (1.5 - 0.5 * pivots * scale * scale)
        at = slice(k + 8 * s, k + 8 * s + 8)
        for (name, h), v in rows[s].items():
            (m_ref if name == "m" else x_ref)[h, at, :] = v * scale
        yield


def trailing_step(k, m_ref, x_ref):
    end = k + PANEL
    if end >= RANK:
        return
    m_halves = [h for h in (0, 1) if 128 * (h + 1) > end]
    x_halves = [h for h in (0, 1) if 128 * h < end]
    scaled = jnp.concatenate([m_ref[h, k:end, :] for h in m_halves], axis=1)
    first = 128 * m_halves[0]
    scaled_t = jnp.transpose(scaled)
    other = jnp.concatenate([x_ref[h, k:end, :] for h in x_halves], axis=1)
    for a, b in ((end, end + PANEL), (end + PANEL, RANK)):
        if a >= b:
            continue
        left = scaled_t[a - first : b - first, :]
        change = dot(left, scaled)
        for n, h in enumerate(m_halves):
            m_ref[h, a:b, :] = m_ref[h, a:b, :] - change[:, 128 * n : 128 * n + 128]
        change = dot(left, other)
        for n, h in enumerate(x_halves):
            x_ref[h, a:b, :] = x_ref[h, a:b, :] - change[:, 128 * n : 128 * n + 128]


def inverse_factor(m_ref, x_ref):
    for k in range(0, RANK, PANEL):
        yield from panel_step(k, m_ref, x_ref)
        trailing_step(k, m_ref, x_ref)
        yield


def kernel(
    grad_ref, momentum_ref, factor_ref,
    out_ref, new_factor_ref, basis_ref, right_high, right_low,
    grad_v, summed, blocks, blocks_t, gathered, part_tiles, part_in, left_tiles, left_t,
    gram_part, gram_in, m_ref, x_ref, product, product_in, passing, right_p, own_right,
    square_part, square_in,
    load_sem, ring_send, ring_recv, pair_send, pair_recv,
    rs_send, rs_recv, half_send, half_recv, ring2_send, ring2_recv, pair2_send, pair2_recv,
    plane_send, plane_recv, line_send, line_recv, sister_send, sister_recv,
    here_y, here_x,
):
    r = lax.axis_index("row")
    c = lax.axis_index("col")
    z = r // 2
    core = lax.rem(r, 2)
    y = c // 4
    x = lax.rem(c, 4)
    sister = (z * 2 + 1 - core, c)

    def ring(d):
        return lax.rem(z + d + 2 * ZN, ZN)

    def along(d):
        return (ring(d) * 2 + core, c)

    def at(zz, k, lo=0, n=OWN):
        return pl.ds(pl.multiple_of(zz * CHIP + k * OWN + lo, 8), n)

    own_load = pltpu.make_async_copy(
        factor_ref, gathered.at[at(z, core), :], load_sem.at[2 * LOADS]
    )
    own_load.start()
    loads = []
    for n in range(LOADS):
        rows = pl.ds(n * (ROWS // LOADS), ROWS // LOADS)
        for m, (src, dst) in enumerate(((grad_ref, grad_v), (momentum_ref, summed))):
            loads.append(
                pltpu.make_async_copy(src.at[rows, :], dst.at[rows, :], load_sem.at[2 * n + m])
            )
    for load in loads:
        load.start()

    barrier = pltpu.get_barrier_semaphore()

    def farthest_first(n, middle):
        return middle + (1 - 2 * lax.rem(n, 2)) * ((n + 1) // 2)

    def each_of_plane(do):
        def some(n, _):
            for dx in (2, 1, 3, 0):
                do(lax.rem(y + farthest_first(n, 4), 8) * 4 + lax.rem(x + dx, 4))
            return 0

        lax.fori_loop(0, 7, some, 0)
        for dx in (2, 1, 3):
            do(y * 4 + lax.rem(x + dx, 4))

    def each_of_line(do):
        def some(n, _):
            for k in range(2):
                do(ring(farthest_first(n, 4)) * 2 + k)
            return 0

        lax.fori_loop(0, 7, some, 0)
        do(z * 2 + 1 - core)

    def greet(device):
        pl.semaphore_signal(barrier, 1, device_id=device, device_id_type=MESH)

    def beside(dy, dx):
        return (r, lax.rem(y + dy, 8) * 4 + lax.rem(x + dx, 4))

    in_y = (2, 6, 1, 7)
    in_x = (2, 1, 3)
    for d in (2, -2, 1, -1):
        greet(along(d))
    for d in in_y:
        greet(beside(d, 0))
    for d in in_x:
        greet(beside(0, d))
    greet(sister)
    pl.semaphore_wait(barrier, 12)

    def tell_y():
        for d in in_y[0:2]:
            pl.semaphore_signal(
                here_y, 1, device_id=beside(d, 0), device_id_type=MESH
            )

    def tell_x():
        pl.semaphore_wait(here_y, 2)
        for d in in_x:
            pl.semaphore_signal(
                here_x, 1, device_id=beside(0, d), device_id_type=MESH
            )

    def pieces(dist, way):
        if dist < 4:
            return range(NS)
        return range(CUT) if way == 0 else range(CUT, NS)

    def ring_gather(buf, own, sends, recvs, psend, precv):
        def hop(way, dist, s):
            lo, n = SUBS[s]
            ref = buf.at[at(ring(-SIGN[way] * PARENT[dist]), core, lo, n), :]
            return pltpu.make_async_remote_copy(
                src_ref=own.at[pl.ds(lo, n), :] if dist == 1 else ref, dst_ref=ref,
                send_sem=sends.at[way, dist - 1, s], recv_sem=recvs.at[way, dist - 1, s],
                device_id=along(SIGN[way] * (dist - PARENT[dist])), device_id_type=MESH,
            )

        def over(way, dist):
            if dist < 4:
                lo, n = 0, OWN
            elif way == 0:
                lo, n = 0, SUBS[CUT][0]
            else:
                lo, n = SUBS[CUT][0], OWN - SUBS[CUT][0]
            ref = buf.at[at(ring(-SIGN[way] * dist), core, lo, n), :]
            return pltpu.make_async_remote_copy(
                src_ref=own if dist == 0 else ref, dst_ref=ref,
                send_sem=psend.at[way, dist], recv_sem=precv.at[way, dist],
                device_id=sister, device_id_type=MESH,
            )

        def start(s):
            for way in (0, 1):
                hop(way, 1, s).start()

        def take(dist, some=range(NS)):
            for s in some:
                for way in (0, 1):
                    if s not in pieces(dist, way):
                        continue
                    hop(way, dist, s).wait_recv()
                    for later in (4, 3, 2):
                        if PARENT[later] == dist and s in pieces(later, way):
                            hop(way, later, s).start()
            for way in (0, 1):
                if pieces(dist, way)[-1] in some:
                    over(way, dist).start()

        def have(dist):
            for way in (0, 1):
                if dist > 0 or way == 0:
                    over(way, dist).wait_recv()

        def finish():
            over(0, 0).wait_send()
            for dist in range(1, 5):
                for way in (0, 1):
                    over(way, dist).wait_send()
                    for s in pieces(dist, way):
                        hop(way, dist, s).wait_send()

        return start, take, have, finish, over

    start, take, have, finish, over = ring_gather(
        gathered, factor_ref, ring_send, ring_recv, pair_send, pair_recv
    )
    for s in range(NS):
        start(s)
    over(0, 0).start()
    tell_y()
    for load in loads:
        load.wait()
    own_load.wait()
    for n in range(0, COLS, 128):
        lanes = slice(n, n + 128)
        summed[:, lanes] = summed[:, lanes] + grad_v[:, lanes]
    for b in range(ZN):
        blocks[b, :, 0:CHIP] = summed[:, b * CHIP : (b + 1) * CHIP]

    def partial(zz):
        return dot(blocks[zz, :, 0:CHIP], gathered[pl.ds(pl.multiple_of(zz * CHIP, 8), CHIP), :])

    take(1)
    tell_x()
    have(0)
    total = partial(z)
    take(2)
    have(1)
    total = total + partial(ring(-1)) + partial(ring(1))
    take(3)
    take(4)
    have(2)
    total = total + partial(ring(-2)) + partial(ring(2))
    have(3)
    total = total + partial(ring(-3)) + partial(ring(3))
    have(4)
    total = total + partial(ring(4))

    pl.semaphore_wait(here_x, 3)
    for h in range(2):
        part_tiles[h] = total[:, 128 * h : 128 * h + 128]

    def tile(ref, q):
        return ref.at[q // 16, pl.ds(pl.multiple_of(lax.rem(q, 16) * 8, 8), 8), :]

    def spread(src, dst, index):
        def send(q):
            pltpu.make_async_remote_copy(
                src_ref=src(q), dst_ref=dst,
                send_sem=plane_send.at[index], recv_sem=plane_recv.at[index],
                device_id=(r, q), device_id_type=MESH,
            ).start()

        each_of_plane(send)

    def plane_wait(sem):
        pltpu.make_async_copy(
            part_in.at[pl.ds(0, CN - 1)], part_in.at[pl.ds(0, CN - 1)], sem
        ).wait()

    spread(lambda q: tile(part_tiles, q), part_in.at[c], 0)
    part_in[c] = part_tiles[c // 16, pl.ds(pl.multiple_of(lax.rem(c, 16) * 8, 8), 8), :]
    for b in range(ZN):
        blocks_t[b] = jnp.transpose(blocks[b, :, 0:CHIP])
    finish()
    plane_wait(plane_recv.at[0])
    own_tile = part_in[0]
    for q in range(1, CN):
        own_tile = own_tile + part_in[q]
    left_tiles[c // 16, pl.ds(pl.multiple_of(lax.rem(c, 16) * 8, 8), 8), :] = own_tile
    spread(lambda q: tile(left_tiles, c), tile(left_tiles, c), 1)
    plane_wait(plane_recv.at[1])
    left = jnp.concatenate([left_tiles[0], left_tiles[1]], axis=1)

    def give(dist):
        zz = ring(dist)
        return pltpu.make_async_remote_copy(
            src_ref=product.at[at(zz, 1 - core), :], dst_ref=product_in.at[zz],
            send_sem=half_send.at[dist], recv_sem=half_recv.at[dist],
            device_id=sister, device_id_type=MESH,
        )

    def multiply(dist):
        zz = ring(dist)
        product[pl.ds(pl.multiple_of(zz * CHIP, 8), CHIP), :] = dot(blocks_t[zz], left)
        give(dist).start()

    def add_sister(dist):
        zz = ring(dist)
        give(dist).wait_recv()
        product[at(zz, core), :] = product[at(zz, core), :] + product_in[zz]

    def onward(way, dist, s):
        lo, n = SUBS[s]
        return pltpu.make_async_remote_copy(
            src_ref=product.at[at(ring(SIGN[way] * dist), core, lo, n), :],
            dst_ref=passing.at[way, dist - 1, pl.ds(lo, n), :],
            send_sem=rs_send.at[way, dist - 1, s], recv_sem=rs_recv.at[way, dist - 1, s],
            device_id=along(SIGN[way] * (dist - PARENT[dist])), device_id_type=MESH,
        )

    def scatter(dist, some):
        for s in some:
            lo, n = SUBS[s]
            for way in (0, 1):
                rows = at(ring(SIGN[way] * dist), core, lo, n)
                value = product[rows, :]
                for earlier in (3, 4, 2, 1):
                    if PARENT[earlier] == dist and s in pieces(earlier, way):
                        onward(way, earlier, s).wait_recv()
                        value = value + passing[way, earlier - 1, lo : lo + n, :]
                product[rows, :] = value
                if dist > 0:
                    onward(way, dist, s).start()
            if dist == 0:
                gather_piece(s)

    def scatter_finish():
        for dist in range(8):
            give(dist).wait_send()
        for dist in range(1, 5):
            for way in (0, 1):
                for s in pieces(dist, way):
                    onward(way, dist, s).wait_send()

    start2, take2, have2, finish2, over2 = ring_gather(
        right_p, right_p.at[at(z, core), :], ring2_send, ring2_recv, pair2_send, pair2_recv
    )

    def gather_piece(s):
        lo, n = SUBS[s]
        rows = at(z, core, lo, n)
        right_p[rows, :] = product[rows, :]
        start2(s)

    for dist in (4, 3, 5):
        multiply(dist)

    for h in range(2):
        left_t[128 * h : 128 * h + 128, :] = jnp.transpose(left_tiles[h])
    gram_rows = dot(left_t[pl.ds(pl.multiple_of(c * 8, 8), 8), :], left)
    for h in range(2):
        gram_part[h] = gram_rows[:, 128 * h : 128 * h + 128]

    def send_line(q):
        pltpu.make_async_remote_copy(
            src_ref=gram_part.at[lax.rem(q, 2)], dst_ref=gram_in.at[r],
            send_sem=line_send, recv_sem=line_recv,
            device_id=(q, c), device_id_type=MESH,
        ).start()

    each_of_line(send_line)
    gram_in[r] = gram_part[core]

    add_sister(4)
    for s in range(CUT):
        onward(0, 4, s).start()
        onward(1, 4, CUT + s).start()
    add_sister(3)
    add_sister(5)
    for s in range(NS):
        for way in (0, 1):
            onward(way, 3, s).start()
    for dist in (2, 6, 1, 7, 0):
        multiply(dist)
    row = lax.broadcasted_iota(jnp.int32, (RANK, HALF), 0)
    lane = lax.broadcasted_iota(jnp.int32, (RANK, HALF), 1)
    for h in range(2):
        x_ref[h] = jnp.where(row == lane + 128 * h, 1.0, 0.0).astype(F32)
    for dist in (2, 6, 1, 7, 0):
        add_sister(dist)

    def line_wait(sem):
        pltpu.make_async_copy(
            gram_in.at[pl.ds(0, RN - 1)], gram_in.at[pl.ds(0, RN - 1)], sem
        ).wait()

    scatter(2, (0, 1))
    line_wait(line_recv)
    gram_tile = gram_in[0]
    for q in range(1, RN):
        gram_tile = gram_tile + gram_in[q]
    gram_at = pl.ds(pl.multiple_of(c * 8, 8), 8)
    m_ref[core, gram_at, :] = gram_tile
    spread(lambda q: m_ref.at[core, gram_at, :], m_ref.at[core, gram_at, :], 2)
    scatter(2, (2, 3))
    scatter(1, range(NS))
    scatter(0, (0, 1))
    plane_wait(plane_recv.at[2])
    to_sister = pltpu.make_async_remote_copy(
        src_ref=m_ref.at[core], dst_ref=m_ref.at[core],
        send_sem=sister_send, recv_sem=sister_recv,
        device_id=sister, device_id_type=MESH,
    )
    to_sister.start()
    scatter(0, (2, 3))
    over2(0, 0).start()
    plane_wait(plane_send.at[2])
    to_sister.wait()

    units = inverse_factor(m_ref, x_ref)

    def advance(count):
        for _ in range(count):
            next(units, None)

    for before, dists in ((2, (1,)), (6, (2,)), (8, (3, 4))):
        advance(before)
        for s in range(NS):
            for dist in dists:
                take2(dist, (s,))
            advance(2)
    for _ in units:
        pass

    inverse = jnp.concatenate([x_ref[0], x_ref[1]], axis=1)

    def right_block(zz, own=False):
        rows = pl.ds(pl.multiple_of(zz * CHIP, 16), CHIP)
        value = dot_t(right_p[rows, :], inverse)
        high, low = split(value)
        right_high[rows, :] = high
        right_low[rows, :] = low
        if own:
            own_right[...] = value
        return jnp.sum((value * value).reshape(CHIP // 8, 8, RANK), axis=0)

    squares = jnp.zeros((8, RANK), F32)
    basis = dot_t(left, inverse)
    for dist in range(5):
        have2(dist)
        if dist == 0:
            squares = squares + right_block(z, own=True)
        elif dist == 4:
            squares = squares + right_block(ring(4))
        else:
            squares = squares + right_block(ring(-dist)) + right_block(ring(dist))
    squares = jnp.sum(squares, axis=0, keepdims=True)
    which = lax.broadcasted_iota(jnp.int32, (8, HALF), 0)
    square_tile = jnp.where(which == 0, squares[:, 0:128], squares[:, 128:256])
    square_part[...] = square_tile
    square_in[c] = square_tile
    spread(lambda q: square_part, square_in.at[c], 3)

    basis_split = split(basis)
    for n in range(0, COLS, 128):
        lanes = slice(n, n + 128)
        right_n = (right_high[lanes, :], right_low[lanes, :])
        out_ref[:, lanes] = summed[:, lanes] - feedback * split_dot_t(basis_split, right_n)
    for index in (0, 1):
        plane_wait(plane_send.at[index])
    line_wait(line_send)
    scatter_finish()
    finish2()

    plane_wait(plane_recv.at[3])
    square_sum = square_in[0]
    for q in range(1, CN):
        square_sum = square_sum + square_in[q]
    norm = jnp.sqrt(square_sum) + epsilon
    norm = jnp.concatenate([norm[0:1, :], norm[1:2, :]], axis=1)
    mine = pl.ds(pl.multiple_of(core * OWN, 8), OWN)
    new_factor_ref[...] = own_right[mine, :] / norm
    multiplier = math.sqrt(ROWS * RN * COLS * CN / RANK)
    basis_ref[...] = basis * (multiplier / norm)
    plane_wait(plane_send.at[3])


def write_kernel(
    momentum_v, factor_v, basis_ref, right_high, right_low, update_ref, out_ref, new_factor_ref,
    update_v, sems,
):
    copies = [pltpu.make_async_copy(factor_v, new_factor_ref, sems.at[0])]
    step = ROWS // LOADS
    for n in range(LOADS):
        rows = pl.ds(n * step, step)
        copies.append(
            pltpu.make_async_copy(momentum_v.at[rows, :], out_ref.at[rows, :], sems.at[1 + n])
        )
    for copy in copies:
        copy.start()
    basis = split(basis_ref[...])
    for i, n in enumerate(range(0, COLS, 128)):
        lanes = slice(n, n + 128)
        update_v[:, lanes] = split_dot_t(basis, (right_high[lanes, :], right_low[lanes, :]))
        copy = pltpu.make_async_copy(
            update_v.at[:, pl.ds(n, 128)], update_ref.at[:, pl.ds(n, 128)], sems.at[1 + LOADS + i]
        )
        copy.start()
        copies.append(copy)
    for copy in copies:
        copy.wait()


def per_device(grad, momentum, factor):
    vmem = pl.BlockSpec(memory_space=pltpu.VMEM)
    hbm = pl.BlockSpec(memory_space=pltpu.HBM)
    dma = pltpu.SemaphoreType.DMA
    out_shape = (
        jax.ShapeDtypeStruct((ROWS, COLS), F32),
        jax.ShapeDtypeStruct((OWN, RANK), F32),
        jax.ShapeDtypeStruct((ROWS, RANK), F32),
        jax.ShapeDtypeStruct((COLS, RANK), BF16),
        jax.ShapeDtypeStruct((COLS, RANK), BF16),
    )
    scratch = [
        pltpu.VMEM((ROWS, COLS), F32),
        pltpu.VMEM((ROWS, COLS), F32),
        pltpu.VMEM((ZN, ROWS, 256), F32),
        pltpu.VMEM((ZN, CHIP, ROWS), F32),
        pltpu.VMEM((COLS, RANK), F32),
        pltpu.VMEM((2, ROWS, HALF), F32),
        pltpu.VMEM((CN, 8, HALF), F32),
        pltpu.VMEM((2, ROWS, HALF), F32),
        pltpu.VMEM((RANK, ROWS), F32),
        pltpu.VMEM((2, 8, HALF), F32),
        pltpu.VMEM((RN, 8, HALF), F32),
        pltpu.VMEM((2, RANK, HALF), F32),
        pltpu.VMEM((2, RANK, HALF), F32),
        pltpu.VMEM((COLS, RANK), F32),
        pltpu.VMEM((ZN, OWN, RANK), F32),
        pltpu.VMEM((2, 4, OWN, RANK), F32),
        pltpu.VMEM((COLS, RANK), F32),
        pltpu.VMEM((CHIP, RANK), F32),
        pltpu.VMEM((8, HALF), F32),
        pltpu.VMEM((CN, 8, HALF), F32),
        dma((2 * LOADS + 1,)),
        dma((2, 4, NS)), dma((2, 4, NS)),
        dma((2, 5)), dma((2, 5)),
        dma((2, 4, NS)), dma((2, 4, NS)),
        dma((8,)), dma((8,)),
        dma((2, 4, NS)), dma((2, 4, NS)),
        dma((2, 5)), dma((2, 5)),
        dma((4,)), dma((4,)),
        dma, dma,
        dma, dma,
        pltpu.SemaphoreType.REGULAR, pltpu.SemaphoreType.REGULAR,
    ]
    sent = pl.pallas_call(
        kernel,
        out_shape=out_shape,
        in_specs=[hbm, hbm, hbm],
        out_specs=(vmem,) * 5,
        scratch_shapes=scratch,
        compiler_params=pltpu.CompilerParams(
            collective_id=0, has_side_effects=True, vmem_limit_bytes=52224 * 1024
        ),
    )(grad, momentum, factor)
    full = jax.ShapeDtypeStruct((ROWS, COLS), F32)
    return pl.pallas_call(
        write_kernel,
        out_shape=(full, full, jax.ShapeDtypeStruct((OWN, RANK), F32)),
        in_specs=[vmem] * 5,
        out_specs=(hbm,) * 3,
        scratch_shapes=[pltpu.VMEM((ROWS, COLS), F32), dma((1 + LOADS + COLS // 128,))],
        compiler_params=pltpu.CompilerParams(vmem_limit_bytes=16 * 1024 * 1024),
    )(*sent)


def solution(mesh):
    return jax.shard_map(
        per_device,
        mesh=mesh,
        in_specs=(P("row", "col"), P("row", "col"), P(("col", "row"), None)),
        out_specs=(P("row", "col"), P("row", "col"), P(("col", "row"), None)),
        check_vma=False,
    )
```

```python
import functools
import math

import jax
import jax.numpy as jnp
from jax import lax
from jax.experimental import pallas as pl
from jax.experimental.pallas import tpu as pltpu
from jax.sharding import PartitionSpec as P

feedback = 0.05
epsilon = 1e-06
MESH = pl.DeviceIdType.MESH
HIGHEST = lax.Precision.HIGHEST
F32 = jnp.float32
BF16 = jnp.bfloat16

RANK = 256
HALF = 128
ZN = 8
RN = 16
CN = 32
ROWS = 128
COLS = 1664
OWN = COLS // RN
CHIP = 2 * OWN
SUBS = ((0, 32), (32, 24), (56, 24), (80, 24))
NS = len(SUBS)
CUT = 2
PARENT = {1: 0, 2: 1, 3: 2, 4: 2}
SIGN = (1, -1)
LOADS = 4
PANEL = 32


def dot(a, b):
    return jnp.dot(a, b, precision=HIGHEST, preferred_element_type=F32)


def dot_t(a, b):
    return lax.dot_general(
        a, b, (((1,), (1,)), ((), ())), precision=HIGHEST, preferred_element_type=F32
    )


def split(a):
    high = a.astype(BF16)
    return high, (a - high.astype(F32)).astype(BF16)


def split3(a):
    high = a.astype(BF16)
    rest = a - high.astype(F32)
    middle = rest.astype(BF16)
    return high, middle, (rest - middle.astype(F32)).astype(BF16)


def split3_dot(a, b):
    def part(x, y):
        return jnp.dot(x, y, preferred_element_type=F32)

    small = (part(a[1], b[1]) + part(a[0], b[2])) + part(a[2], b[0])
    return part(a[0], b[0]) + ((part(a[0], b[1]) + part(a[1], b[0])) + small)


def split_dot_t(a, b):
    def part(x, y):
        return lax.dot_general(x, y, (((1,), (1,)), ((), ())), preferred_element_type=F32)

    return part(a[0], b[0]) + (part(a[0], b[1]) + part(a[1], b[0]))


def across_rows(x, t):
    return jnp.broadcast_to(x[t : t + 1, :], (8, 128))


def across_lanes(x, t):
    return jnp.broadcast_to(x[:, t : t + 1], (8, 128))


def reciprocal(p):
    r = pltpu.reciprocal(p, approx=True)
    return r * (2.0 - p * r)


def panel_step(k, m_ref, x_ref):
    groups = PANEL // 8
    row = lax.broadcasted_iota(jnp.int32, (8, 128), 0)
    m_halves = [h for h in (0, 1) if 128 * (h + 1) > k]
    x_halves = [h for h in (0, 1) if 128 * h < k + PANEL]
    rows = []
    for g in range(groups):
        at = slice(k + 8 * g, k + 8 * g + 8)
        held = {}
        for h in m_halves:
            held["m", h] = m_ref[h, at, :]
        for h in x_halves:
            held["x", h] = x_ref[h, at, :]
        rows.append(held)
    for s in range(groups):
        base = k + 8 * s
        half, lane = ("m", base // 128), base % 128
        column = [
            [across_lanes(rows[g][half], lane + t) for t in range(8)] if g >= s else None
            for g in range(groups)
        ]
        pivots = jnp.zeros((8, 128), F32)
        for t in range(8):
            pivot = across_rows(column[s][t], t)
            inverse = reciprocal(pivot)
            pivots = jnp.where(row == t, pivot, pivots)
            pivot_row = {h: across_rows(v, t) for h, v in rows[s].items()}
            entry = [across_rows(column[s][j], t) if j > t else None for j in range(8)]
            for g in range(s, groups):
                factor = column[g][t] * inverse
                if g == s:
                    factor = jnp.where(row > t, factor, 0.0)
                for j in range(t + 1, 8):
                    column[g][j] = column[g][j] - factor * entry[j]
                for h in rows[g]:
                    rows[g][h] = rows[g][h] - factor * pivot_row[h]
        scale = lax.rsqrt(pivots)
        scale = scale * (1.5 - 0.5 * pivots * scale * scale)
        at = slice(k + 8 * s, k + 8 * s + 8)
        for (name, h), v in rows[s].items():
            (m_ref if name == "m" else x_ref)[h, at, :] = v * scale
        yield


def trailing_step(k, m_ref, x_ref):
    end = k + PANEL
    if end >= RANK:
        return
    m_halves = [h for h in (0, 1) if 128 * (h + 1) > end]
    x_halves = [h for h in (0, 1) if 128 * h < end]
    scaled = jnp.concatenate([m_ref[h, k:end, :] for h in m_halves], axis=1)
    first = 128 * m_halves[0]
    scaled_t = jnp.transpose(scaled)
    other = jnp.concatenate([x_ref[h, k:end, :] for h in x_halves], axis=1)
    for a, b in ((end, end + PANEL), (end + PANEL, RANK)):
        if a >= b:
            continue
        left = scaled_t[a - first : b - first, :]
        change = dot(left, scaled)
        for n, h in enumerate(m_halves):
            m_ref[h, a:b, :] = m_ref[h, a:b, :] - change[:, 128 * n : 128 * n + 128]
        change = dot(left, other)
        for n, h in enumerate(x_halves):
            x_ref[h, a:b, :] = x_ref[h, a:b, :] - change[:, 128 * n : 128 * n + 128]


def inverse_factor(m_ref, x_ref):
    for k in range(0, RANK, PANEL):
        yield from panel_step(k, m_ref, x_ref)
        trailing_step(k, m_ref, x_ref)
        yield


def kernel(
    grad_ref, momentum_ref, factor_ref,
    out_ref, new_factor_ref, basis_ref, right_high, right_low,
    grad_v, summed, blocks, blocks_t, gathered, part_tiles, part_in, left_tiles, left_t,
    gram_part, gram_in, m_ref, x_ref, product, product_in, passing, right_p, own_right,
    square_part, square_in,
    load_sem, ring_send, ring_recv, pair_send, pair_recv,
    rs_send, rs_recv, half_send, half_recv, ring2_send, ring2_recv, pair2_send, pair2_recv,
    plane_send, plane_recv, line_send, line_recv, sister_send, sister_recv,
    here_y, here_x,
):
    r = lax.axis_index("row")
    c = lax.axis_index("col")
    z = r // 2
    core = lax.rem(r, 2)
    y = c // 4
    x = lax.rem(c, 4)
    sister = (z * 2 + 1 - core, c)

    def ring(d):
        return lax.rem(z + d + 2 * ZN, ZN)

    def along(d):
        return (ring(d) * 2 + core, c)

    def at(zz, k, lo=0, n=OWN):
        return pl.ds(pl.multiple_of(zz * CHIP + k * OWN + lo, 8), n)

    own_load = pltpu.make_async_copy(
        factor_ref, gathered.at[at(z, core), :], load_sem.at[2 * LOADS]
    )
    own_load.start()
    loads = []
    for n in range(LOADS):
        rows = pl.ds(n * (ROWS // LOADS), ROWS // LOADS)
        for m, (src, dst) in enumerate(((grad_ref, grad_v), (momentum_ref, summed))):
            loads.append(
                pltpu.make_async_copy(src.at[rows, :], dst.at[rows, :], load_sem.at[2 * n + m])
            )
    for load in loads:
        load.start()

    barrier = pltpu.get_barrier_semaphore()

    def farthest_first(n, middle):
        return middle + (1 - 2 * lax.rem(n, 2)) * ((n + 1) // 2)

    def each_of_plane(do):
        def some(n, _):
            for dx in (2, 1, 3, 0):
                do(lax.rem(y + farthest_first(n, 4), 8) * 4 + lax.rem(x + dx, 4))
            return 0

        lax.fori_loop(0, 7, some, 0)
        for dx in (2, 1, 3):
            do(y * 4 + lax.rem(x + dx, 4))

    def each_of_line(do):
        def some(n, _):
            for k in range(2):
                do(ring(farthest_first(n, 4)) * 2 + k)
            return 0

        lax.fori_loop(0, 7, some, 0)
        do(z * 2 + 1 - core)

    def greet(device):
        pl.semaphore_signal(barrier, 1, device_id=device, device_id_type=MESH)

    def beside(dy, dx):
        return (r, lax.rem(y + dy, 8) * 4 + lax.rem(x + dx, 4))

    in_y = (2, 6, 1, 7)
    in_x = (2, 1, 3)
    for d in (2, -2, 1, -1):
        greet(along(d))
    for d in in_y:
        greet(beside(d, 0))
    for d in in_x:
        greet(beside(0, d))
    greet(sister)
    pl.semaphore_wait(barrier, 12)

    def tell_y():
        for d in in_y[0:2]:
            pl.semaphore_signal(
                here_y, 1, device_id=beside(d, 0), device_id_type=MESH
            )

    def tell_x():
        pl.semaphore_wait(here_y, 2)
        for d in in_x:
            pl.semaphore_signal(
                here_x, 1, device_id=beside(0, d), device_id_type=MESH
            )

    def pieces(dist, way):
        if dist < 4:
            return range(NS)
        return range(CUT) if way == 0 else range(CUT, NS)

    def ring_gather(buf, own, sends, recvs, psend, precv):
        def hop(way, dist, s):
            lo, n = SUBS[s]
            ref = buf.at[at(ring(-SIGN[way] * PARENT[dist]), core, lo, n), :]
            return pltpu.make_async_remote_copy(
                src_ref=own.at[pl.ds(lo, n), :] if dist == 1 else ref, dst_ref=ref,
                send_sem=sends.at[way, dist - 1, s], recv_sem=recvs.at[way, dist - 1, s],
                device_id=along(SIGN[way] * (dist - PARENT[dist])), device_id_type=MESH,
            )

        def over(way, dist):
            if dist < 4:
                lo, n = 0, OWN
            elif way == 0:
                lo, n = 0, SUBS[CUT][0]
            else:
                lo, n = SUBS[CUT][0], OWN - SUBS[CUT][0]
            ref = buf.at[at(ring(-SIGN[way] * dist), core, lo, n), :]
            return pltpu.make_async_remote_copy(
                src_ref=own if dist == 0 else ref, dst_ref=ref,
                send_sem=psend.at[way, dist], recv_sem=precv.at[way, dist],
                device_id=sister, device_id_type=MESH,
            )

        def start(s):
            for way in (0, 1):
                hop(way, 1, s).start()

        def take(dist, some=range(NS)):
            for s in some:
                for way in (0, 1):
                    if s not in pieces(dist, way):
                        continue
                    hop(way, dist, s).wait_recv()
                    for later in (4, 3, 2):
                        if PARENT[later] == dist and s in pieces(later, way):
                            hop(way, later, s).start()
            for way in (0, 1):
                if pieces(dist, way)[-1] in some:
                    over(way, dist).start()

        def have(dist):
            for way in (0, 1):
                if dist > 0 or way == 0:
                    over(way, dist).wait_recv()

        def finish():
            over(0, 0).wait_send()
            for dist in range(1, 5):
                for way in (0, 1):
                    over(way, dist).wait_send()
                    for s in pieces(dist, way):
                        hop(way, dist, s).wait_send()

        return start, take, have, finish, over

    start, take, have, finish, over = ring_gather(
        gathered, factor_ref, ring_send, ring_recv, pair_send, pair_recv
    )
    for s in range(NS):
        start(s)
    over(0, 0).start()
    tell_y()
    for load in loads:
        load.wait()
    own_load.wait()
    for n in range(0, COLS, 128):
        lanes = slice(n, n + 128)
        summed[:, lanes] = summed[:, lanes] + grad_v[:, lanes]
    for b in range(ZN):
        blocks[b, :, 0:CHIP] = summed[:, b * CHIP : (b + 1) * CHIP]

    def partial(zz):
        return dot(blocks[zz, :, 0:CHIP], gathered[pl.ds(pl.multiple_of(zz * CHIP, 8), CHIP), :])

    take(1)
    tell_x()
    have(0)
    total = partial(z)
    take(2)
    have(1)
    total = total + partial(ring(-1)) + partial(ring(1))
    take(3)
    take(4)
    have(2)
    total = total + partial(ring(-2)) + partial(ring(2))
    have(3)
    total = total + partial(ring(-3)) + partial(ring(3))
    have(4)
    total = total + partial(ring(4))

    pl.semaphore_wait(here_x, 3)
    for h in range(2):
        part_tiles[h] = total[:, 128 * h : 128 * h + 128]

    def tile(ref, q):
        return ref.at[q // 16, pl.ds(pl.multiple_of(lax.rem(q, 16) * 8, 8), 8), :]

    def spread(src, dst, index):
        def send(q):
            pltpu.make_async_remote_copy(
                src_ref=src(q), dst_ref=dst,
                send_sem=plane_send.at[index], recv_sem=plane_recv.at[index],
                device_id=(r, q), device_id_type=MESH,
            ).start()

        each_of_plane(send)

    def plane_wait(sem):
        pltpu.make_async_copy(
            part_in.at[pl.ds(0, CN - 1)], part_in.at[pl.ds(0, CN - 1)], sem
        ).wait()

    spread(lambda q: tile(part_tiles, q), part_in.at[c], 0)
    part_in[c] = part_tiles[c // 16, pl.ds(pl.multiple_of(lax.rem(c, 16) * 8, 8), 8), :]
    for b in range(ZN):
        blocks_t[b] = jnp.transpose(blocks[b, :, 0:CHIP])
    finish()
    plane_wait(plane_recv.at[0])
    own_tile = part_in[0]
    for q in range(1, CN):
        own_tile = own_tile + part_in[q]
    left_tiles[c // 16, pl.ds(pl.multiple_of(lax.rem(c, 16) * 8, 8), 8), :] = own_tile
    spread(lambda q: tile(left_tiles, c), tile(left_tiles, c), 1)
    plane_wait(plane_recv.at[1])
    left = jnp.concatenate([left_tiles[0], left_tiles[1]], axis=1)

    def give(dist):
        zz = ring(dist)
        return pltpu.make_async_remote_copy(
            src_ref=product.at[at(zz, 1 - core), :], dst_ref=product_in.at[zz],
            send_sem=half_send.at[dist], recv_sem=half_recv.at[dist],
            device_id=sister, device_id_type=MESH,
        )

    def multiply(dist):
        zz = ring(dist)
        product[pl.ds(pl.multiple_of(zz * CHIP, 8), CHIP), :] = dot(blocks_t[zz], left)
        give(dist).start()

    def add_sister(dist):
        zz = ring(dist)
        give(dist).wait_recv()
        product[at(zz, core), :] = product[at(zz, core), :] + product_in[zz]

    def onward(way, dist, s):
        lo, n = SUBS[s]
        return pltpu.make_async_remote_copy(
            src_ref=product.at[at(ring(SIGN[way] * dist), core, lo, n), :],
            dst_ref=passing.at[way, dist - 1, pl.ds(lo, n), :],
            send_sem=rs_send.at[way, dist - 1, s], recv_sem=rs_recv.at[way, dist - 1, s],
            device_id=along(SIGN[way] * (dist - PARENT[dist])), device_id_type=MESH,
        )

    def scatter(dist, some):
        for s in some:
            lo, n = SUBS[s]
            for way in (0, 1):
                rows = at(ring(SIGN[way] * dist), core, lo, n)
                value = product[rows, :]
                for earlier in (3, 4, 2, 1):
                    if PARENT[earlier] == dist and s in pieces(earlier, way):
                        onward(way, earlier, s).wait_recv()
                        value = value + passing[way, earlier - 1, lo : lo + n, :]
                product[rows, :] = value
                if dist > 0:
                    onward(way, dist, s).start()
            if dist == 0:
                gather_piece(s)

    def scatter_finish():
        for dist in range(8):
            give(dist).wait_send()
        for dist in range(1, 5):
            for way in (0, 1):
                for s in pieces(dist, way):
                    onward(way, dist, s).wait_send()

    start2, take2, have2, finish2, over2 = ring_gather(
        right_p, right_p.at[at(z, core), :], ring2_send, ring2_recv, pair2_send, pair2_recv
    )

    def gather_piece(s):
        lo, n = SUBS[s]
        rows = at(z, core, lo, n)
        right_p[rows, :] = product[rows, :]
        start2(s)

    for dist in (4, 3, 5):
        multiply(dist)

    for h in range(2):
        left_t[128 * h : 128 * h + 128, :] = jnp.transpose(left_tiles[h])
    gram_rows = dot(left_t[pl.ds(pl.multiple_of(c * 8, 8), 8), :], left)
    for h in range(2):
        gram_part[h] = gram_rows[:, 128 * h : 128 * h + 128]

    def send_line(q):
        pltpu.make_async_remote_copy(
            src_ref=gram_part.at[lax.rem(q, 2)], dst_ref=gram_in.at[r],
            send_sem=line_send, recv_sem=line_recv,
            device_id=(q, c), device_id_type=MESH,
        ).start()

    each_of_line(send_line)
    gram_in[r] = gram_part[core]

    for dist in (4, 3, 5):
        add_sister(dist)
    for s in range(NS):
        for way in (0, 1):
            if s in pieces(4, way):
                onward(way, 4, s).start()
            onward(way, 3, s).start()
    for dist in (2, 6, 1, 7, 0):
        multiply(dist)
    row = lax.broadcasted_iota(jnp.int32, (RANK, HALF), 0)
    lane = lax.broadcasted_iota(jnp.int32, (RANK, HALF), 1)
    for h in range(2):
        x_ref[h] = jnp.where(row == lane + 128 * h, 1.0, 0.0).astype(F32)
    for dist in (2, 6, 1, 7, 0):
        add_sister(dist)

    def line_wait(sem):
        pltpu.make_async_copy(
            gram_in.at[pl.ds(0, RN - 1)], gram_in.at[pl.ds(0, RN - 1)], sem
        ).wait()

    scatter(2, (0, 1))
    line_wait(line_recv)
    gram_tile = gram_in[0]
    for q in range(1, RN):
        gram_tile = gram_tile + gram_in[q]
    gram_at = pl.ds(pl.multiple_of(c * 8, 8), 8)
    m_ref[core, gram_at, :] = gram_tile
    spread(lambda q: m_ref.at[core, gram_at, :], m_ref.at[core, gram_at, :], 2)
    scatter(2, (2, 3))
    scatter(1, range(NS))
    scatter(0, (0, 1))
    plane_wait(plane_recv.at[2])
    to_sister = pltpu.make_async_remote_copy(
        src_ref=m_ref.at[core], dst_ref=m_ref.at[core],
        send_sem=sister_send, recv_sem=sister_recv,
        device_id=sister, device_id_type=MESH,
    )
    to_sister.start()
    scatter(0, (2, 3))
    over2(0, 0).start()
    plane_wait(plane_send.at[2])
    to_sister.wait()

    units = inverse_factor(m_ref, x_ref)

    def advance(count):
        for _ in range(count):
            next(units, None)

    for before, dists in ((2, (1,)), (6, (2,)), (8, (3, 4))):
        advance(before)
        for s in range(NS):
            for dist in dists:
                take2(dist, (s,))
            advance(2)
    for _ in units:
        pass

    inverse = jnp.concatenate([x_ref[0], x_ref[1]], axis=1)

    inverse_t = split3(jnp.transpose(inverse))

    def right_block(zz, own=False):
        rows = pl.ds(pl.multiple_of(zz * CHIP, 16), CHIP)
        value = split3_dot(split3(right_p[rows, :]), inverse_t)
        high, low = split(value)
        right_high[rows, :] = high
        right_low[rows, :] = low
        if own:
            own_right[...] = value
        return jnp.sum((value * value).reshape(CHIP // 8, 8, RANK), axis=0)

    squares = jnp.zeros((8, RANK), F32)
    basis = dot_t(left, inverse)
    for dist in range(5):
        have2(dist)
        if dist == 0:
            squares = squares + right_block(z, own=True)
        elif dist == 4:
            squares = squares + right_block(ring(4))
        else:
            squares = squares + right_block(ring(-dist)) + right_block(ring(dist))
    squares = jnp.sum(squares, axis=0, keepdims=True)
    which = lax.broadcasted_iota(jnp.int32, (8, HALF), 0)
    square_tile = jnp.where(which == 0, squares[:, 0:128], squares[:, 128:256])
    square_part[...] = square_tile
    square_in[c] = square_tile
    spread(lambda q: square_part, square_in.at[c], 3)

    basis_split = split(basis)
    for n in range(0, COLS, 128):
        lanes = slice(n, n + 128)
        right_n = (right_high[lanes, :], right_low[lanes, :])
        out_ref[:, lanes] = summed[:, lanes] - feedback * split_dot_t(basis_split, right_n)
    for index in (0, 1):
        plane_wait(plane_send.at[index])
    line_wait(line_send)
    scatter_finish()
    finish2()

    plane_wait(plane_recv.at[3])
    square_sum = square_in[0]
    for q in range(1, CN):
        square_sum = square_sum + square_in[q]
    norm = jnp.sqrt(square_sum) + epsilon
    norm = jnp.concatenate([norm[0:1, :], norm[1:2, :]], axis=1)
    mine = pl.ds(pl.multiple_of(core * OWN, 8), OWN)
    new_factor_ref[...] = own_right[mine, :] / norm
    multiplier = math.sqrt(ROWS * RN * COLS * CN / RANK)
    basis_ref[...] = basis * (multiplier / norm)
    plane_wait(plane_send.at[3])


def write_kernel(
    momentum_v, factor_v, basis_ref, right_high, right_low, update_ref, out_ref, new_factor_ref,
    update_v, sems,
):
    copies = [pltpu.make_async_copy(factor_v, new_factor_ref, sems.at[0])]
    step = ROWS // LOADS
    for n in range(LOADS):
        rows = pl.ds(n * step, step)
        copies.append(
            pltpu.make_async_copy(momentum_v.at[rows, :], out_ref.at[rows, :], sems.at[1 + n])
        )
    for copy in copies:
        copy.start()
    basis = split(basis_ref[...])
    for i, n in enumerate(range(0, COLS, 128)):
        lanes = slice(n, n + 128)
        update_v[:, lanes] = split_dot_t(basis, (right_high[lanes, :], right_low[lanes, :]))
        copy = pltpu.make_async_copy(
            update_v.at[:, pl.ds(n, 128)], update_ref.at[:, pl.ds(n, 128)], sems.at[1 + LOADS + i]
        )
        copy.start()
        copies.append(copy)
    for copy in copies:
        copy.wait()


def per_device(grad, momentum, factor):
    vmem = pl.BlockSpec(memory_space=pltpu.VMEM)
    hbm = pl.BlockSpec(memory_space=pltpu.HBM)
    dma = pltpu.SemaphoreType.DMA
    out_shape = (
        jax.ShapeDtypeStruct((ROWS, COLS), F32),
        jax.ShapeDtypeStruct((OWN, RANK), F32),
        jax.ShapeDtypeStruct((ROWS, RANK), F32),
        jax.ShapeDtypeStruct((COLS, RANK), BF16),
        jax.ShapeDtypeStruct((COLS, RANK), BF16),
    )
    scratch = [
        pltpu.VMEM((ROWS, COLS), F32),
        pltpu.VMEM((ROWS, COLS), F32),
        pltpu.VMEM((ZN, ROWS, 256), F32),
        pltpu.VMEM((ZN, CHIP, ROWS), F32),
        pltpu.VMEM((COLS, RANK), F32),
        pltpu.VMEM((2, ROWS, HALF), F32),
        pltpu.VMEM((CN, 8, HALF), F32),
        pltpu.VMEM((2, ROWS, HALF), F32),
        pltpu.VMEM((RANK, ROWS), F32),
        pltpu.VMEM((2, 8, HALF), F32),
        pltpu.VMEM((RN, 8, HALF), F32),
        pltpu.VMEM((2, RANK, HALF), F32),
        pltpu.VMEM((2, RANK, HALF), F32),
        pltpu.VMEM((COLS, RANK), F32),
        pltpu.VMEM((ZN, OWN, RANK), F32),
        pltpu.VMEM((2, 4, OWN, RANK), F32),
        pltpu.VMEM((COLS, RANK), F32),
        pltpu.VMEM((CHIP, RANK), F32),
        pltpu.VMEM((8, HALF), F32),
        pltpu.VMEM((CN, 8, HALF), F32),
        dma((2 * LOADS + 1,)),
        dma((2, 4, NS)), dma((2, 4, NS)),
        dma((2, 5)), dma((2, 5)),
        dma((2, 4, NS)), dma((2, 4, NS)),
        dma((8,)), dma((8,)),
        dma((2, 4, NS)), dma((2, 4, NS)),
        dma((2, 5)), dma((2, 5)),
        dma((4,)), dma((4,)),
        dma, dma,
        dma, dma,
        pltpu.SemaphoreType.REGULAR, pltpu.SemaphoreType.REGULAR,
    ]
    sent = pl.pallas_call(
        kernel,
        out_shape=out_shape,
        in_specs=[hbm, hbm, hbm],
        out_specs=(vmem,) * 5,
        scratch_shapes=scratch,
        compiler_params=pltpu.CompilerParams(
            collective_id=0, has_side_effects=True, vmem_limit_bytes=52224 * 1024
        ),
    )(grad, momentum, factor)
    full = jax.ShapeDtypeStruct((ROWS, COLS), F32)
    return pl.pallas_call(
        write_kernel,
        out_shape=(full, full, jax.ShapeDtypeStruct((OWN, RANK), F32)),
        in_specs=[vmem] * 5,
        out_specs=(hbm,) * 3,
        scratch_shapes=[pltpu.VMEM((ROWS, COLS), F32), dma((1 + LOADS + COLS // 128,))],
        compiler_params=pltpu.CompilerParams(vmem_limit_bytes=16 * 1024 * 1024),
    )(*sent)


def solution(mesh):
    return jax.shard_map(
        per_device,
        mesh=mesh,
        in_specs=(P("row", "col"), P("row", "col"), P(("col", "row"), None)),
        out_specs=(P("row", "col"), P("row", "col"), P(("col", "row"), None)),
        check_vma=False,
    )
```

```python
import functools
import math

import jax
import jax.numpy as jnp
from jax import lax
from jax.experimental import pallas as pl
from jax.experimental.pallas import tpu as pltpu
from jax.sharding import PartitionSpec as P

feedback = 0.05
epsilon = 1e-06
MESH = pl.DeviceIdType.MESH
HIGHEST = lax.Precision.HIGHEST
F32 = jnp.float32
BF16 = jnp.bfloat16

RANK = 256
HALF = 128
ZN = 8
RN = 16
CN = 32
ROWS = 128
COLS = 1664
OWN = COLS // RN
CHIP = 2 * OWN
SUBS = ((0, 32), (32, 24), (56, 24), (80, 24))
NS = len(SUBS)
CUT = 2
PARENT = {1: 0, 2: 1, 3: 2, 4: 2}
SIGN = (1, -1)
LOADS = 4
PANEL = 32


def dot(a, b):
    return jnp.dot(a, b, precision=HIGHEST, preferred_element_type=F32)


def dot_t(a, b):
    return lax.dot_general(
        a, b, (((1,), (1,)), ((), ())), precision=HIGHEST, preferred_element_type=F32
    )


def split(a):
    high = a.astype(BF16)
    return high, (a - high.astype(F32)).astype(BF16)


def split3(a):
    high = a.astype(BF16)
    rest = a - high.astype(F32)
    middle = rest.astype(BF16)
    return high, middle, (rest - middle.astype(F32)).astype(BF16)


def split3_dot(a, b):
    def part(x, y):
        return jnp.dot(x, y, preferred_element_type=F32)

    small = (part(a[1], b[1]) + part(a[0], b[2])) + part(a[2], b[0])
    return part(a[0], b[0]) + ((part(a[0], b[1]) + part(a[1], b[0])) + small)


def split_dot_t(a, b):
    def part(x, y):
        return lax.dot_general(x, y, (((1,), (1,)), ((), ())), preferred_element_type=F32)

    return part(a[0], b[0]) + (part(a[0], b[1]) + part(a[1], b[0]))


def across_rows(x, t):
    return jnp.broadcast_to(x[t : t + 1, :], (8, 128))


def across_lanes(x, t):
    return jnp.broadcast_to(x[:, t : t + 1], (8, 128))


def reciprocal(p):
    r = pltpu.reciprocal(p, approx=True)
    return r * (2.0 - p * r)


def panel_step(k, m_ref, x_ref):
    groups = PANEL // 8
    row = lax.broadcasted_iota(jnp.int32, (8, 128), 0)
    m_halves = [h for h in (0, 1) if 128 * (h + 1) > k]
    x_halves = [h for h in (0, 1) if 128 * h < k + PANEL]
    rows = []
    for g in range(groups):
        at = slice(k + 8 * g, k + 8 * g + 8)
        held = {}
        for h in m_halves:
            held["m", h] = m_ref[h, at, :]
        for h in x_halves:
            held["x", h] = x_ref[h, at, :]
        rows.append(held)
    for s in range(groups):
        base = k + 8 * s
        half, lane = ("m", base // 128), base % 128
        column = [
            [across_lanes(rows[g][half], lane + t) for t in range(8)] if g >= s else None
            for g in range(groups)
        ]
        pivots = jnp.zeros((8, 128), F32)
        for t in range(8):
            pivot = across_rows(column[s][t], t)
            inverse = reciprocal(pivot)
            pivots = jnp.where(row == t, pivot, pivots)
            pivot_row = {h: across_rows(v, t) for h, v in rows[s].items()}
            entry = [across_rows(column[s][j], t) if j > t else None for j in range(8)]
            for g in range(s, groups):
                factor = column[g][t] * inverse
                if g == s:
                    factor = jnp.where(row > t, factor, 0.0)
                for j in range(t + 1, 8):
                    column[g][j] = column[g][j] - factor * entry[j]
                for h in rows[g]:
                    rows[g][h] = rows[g][h] - factor * pivot_row[h]
        scale = lax.rsqrt(pivots)
        scale = scale * (1.5 - 0.5 * pivots * scale * scale)
        at = slice(k + 8 * s, k + 8 * s + 8)
        for (name, h), v in rows[s].items():
            (m_ref if name == "m" else x_ref)[h, at, :] = v * scale
        yield


def trailing_step(k, m_ref, x_ref):
    end = k + PANEL
    if end >= RANK:
        return
    m_halves = [h for h in (0, 1) if 128 * (h + 1) > end]
    x_halves = [h for h in (0, 1) if 128 * h < end]
    scaled = jnp.concatenate([m_ref[h, k:end, :] for h in m_halves], axis=1)
    first = 128 * m_halves[0]
    scaled_t = jnp.transpose(scaled)
    other = jnp.concatenate([x_ref[h, k:end, :] for h in x_halves], axis=1)
    for a, b in ((end, end + PANEL), (end + PANEL, RANK)):
        if a >= b:
            continue
        left = scaled_t[a - first : b - first, :]
        change = dot(left, scaled)
        for n, h in enumerate(m_halves):
            m_ref[h, a:b, :] = m_ref[h, a:b, :] - change[:, 128 * n : 128 * n + 128]
        change = dot(left, other)
        for n, h in enumerate(x_halves):
            x_ref[h, a:b, :] = x_ref[h, a:b, :] - change[:, 128 * n : 128 * n + 128]


def inverse_factor(m_ref, x_ref):
    for k in range(0, RANK, PANEL):
        yield from panel_step(k, m_ref, x_ref)
        trailing_step(k, m_ref, x_ref)
        yield


def kernel(
    grad_ref, momentum_ref, factor_ref,
    out_ref, new_factor_ref, basis_ref, right_high, right_low,
    grad_v, summed, blocks, blocks_t, gathered, part_tiles, part_in, left_tiles, left_t,
    gram_part, gram_in, m_ref, x_ref, product, product_in, passing, right_p, own_right,
    square_part, square_in,
    load_sem, ring_send, ring_recv, pair_send, pair_recv,
    rs_send, rs_recv, half_send, half_recv, ring2_send, ring2_recv, pair2_send, pair2_recv,
    plane_send, plane_recv, line_send, line_recv, sister_send, sister_recv,
    here_y, here_x,
):
    r = lax.axis_index("row")
    c = lax.axis_index("col")
    z = r // 2
    core = lax.rem(r, 2)
    y = c // 4
    x = lax.rem(c, 4)
    sister = (z * 2 + 1 - core, c)

    def ring(d):
        return lax.rem(z + d + 2 * ZN, ZN)

    def along(d):
        return (ring(d) * 2 + core, c)

    def at(zz, k, lo=0, n=OWN):
        return pl.ds(pl.multiple_of(zz * CHIP + k * OWN + lo, 8), n)

    own_load = pltpu.make_async_copy(
        factor_ref, gathered.at[at(z, core), :], load_sem.at[2 * LOADS]
    )
    own_load.start()
    loads = []
    for n in range(LOADS):
        rows = pl.ds(n * (ROWS // LOADS), ROWS // LOADS)
        for m, (src, dst) in enumerate(((grad_ref, grad_v), (momentum_ref, summed))):
            loads.append(
                pltpu.make_async_copy(src.at[rows, :], dst.at[rows, :], load_sem.at[2 * n + m])
            )
    for load in loads:
        load.start()

    barrier = pltpu.get_barrier_semaphore()

    def farthest_first(n, middle):
        return middle + (1 - 2 * lax.rem(n, 2)) * ((n + 1) // 2)

    def each_of_plane(do):
        def some(n, _):
            for dx in (2, 1, 3, 0):
                do(lax.rem(y + farthest_first(n, 4), 8) * 4 + lax.rem(x + dx, 4))
            return 0

        lax.fori_loop(0, 7, some, 0)
        for dx in (2, 1, 3):
            do(y * 4 + lax.rem(x + dx, 4))

    def each_of_line(do):
        def some(n, _):
            for k in range(2):
                do(ring(farthest_first(n, 4)) * 2 + k)
            return 0

        lax.fori_loop(0, 7, some, 0)
        do(z * 2 + 1 - core)

    def greet(device):
        pl.semaphore_signal(barrier, 1, device_id=device, device_id_type=MESH)

    def beside(dy, dx):
        return (r, lax.rem(y + dy, 8) * 4 + lax.rem(x + dx, 4))

    in_y = (2, 6, 1, 7)
    in_x = (2, 1, 3)
    for d in (2, -2, 1, -1):
        greet(along(d))
    for d in in_y:
        greet(beside(d, 0))
    for d in in_x:
        greet(beside(0, d))
    greet(sister)
    pl.semaphore_wait(barrier, 12)

    def tell_y():
        for d in in_y[0:2]:
            pl.semaphore_signal(
                here_y, 1, device_id=beside(d, 0), device_id_type=MESH
            )

    def tell_x():
        pl.semaphore_wait(here_y, 2)
        for d in in_x:
            pl.semaphore_signal(
                here_x, 1, device_id=beside(0, d), device_id_type=MESH
            )

    def pieces(dist, way):
        if dist < 4:
            return range(NS)
        return range(CUT) if way == 0 else range(CUT, NS)

    def ring_gather(buf, own, sends, recvs, psend, precv):
        def hop(way, dist, s):
            lo, n = SUBS[s]
            ref = buf.at[at(ring(-SIGN[way] * PARENT[dist]), core, lo, n), :]
            return pltpu.make_async_remote_copy(
                src_ref=own.at[pl.ds(lo, n), :] if dist == 1 else ref, dst_ref=ref,
                send_sem=sends.at[way, dist - 1, s], recv_sem=recvs.at[way, dist - 1, s],
                device_id=along(SIGN[way] * (dist - PARENT[dist])), device_id_type=MESH,
            )

        def over(way, dist):
            if dist < 4:
                lo, n = 0, OWN
            elif way == 0:
                lo, n = 0, SUBS[CUT][0]
            else:
                lo, n = SUBS[CUT][0], OWN - SUBS[CUT][0]
            ref = buf.at[at(ring(-SIGN[way] * dist), core, lo, n), :]
            return pltpu.make_async_remote_copy(
                src_ref=own if dist == 0 else ref, dst_ref=ref,
                send_sem=psend.at[way, dist], recv_sem=precv.at[way, dist],
                device_id=sister, device_id_type=MESH,
            )

        def start(s):
            for way in (0, 1):
                hop(way, 1, s).start()

        def take(dist, some=range(NS)):
            for s in some:
                for way in (0, 1):
                    if s not in pieces(dist, way):
                        continue
                    hop(way, dist, s).wait_recv()
                    for later in (4, 3, 2):
                        if PARENT[later] == dist and s in pieces(later, way):
                            hop(way, later, s).start()
            for way in (0, 1):
                if pieces(dist, way)[-1] in some:
                    over(way, dist).start()

        def have(dist):
            for way in (0, 1):
                if dist > 0 or way == 0:
                    over(way, dist).wait_recv()

        def finish():
            over(0, 0).wait_send()
            for dist in range(1, 5):
                for way in (0, 1):
                    over(way, dist).wait_send()
                    for s in pieces(dist, way):
                        hop(way, dist, s).wait_send()

        return start, take, have, finish, over

    start, take, have, finish, over = ring_gather(
        gathered, factor_ref, ring_send, ring_recv, pair_send, pair_recv
    )
    for s in range(NS):
        start(s)
    over(0, 0).start()
    tell_y()
    def partial(zz):
        return dot(blocks[zz, :, 0:CHIP], gathered[pl.ds(pl.multiple_of(zz * CHIP, 8), CHIP), :])

    take(1)
    tell_x()
    for load in loads:
        load.wait()
    own_load.wait()
    for n in range(0, COLS, 128):
        lanes = slice(n, n + 128)
        summed[:, lanes] = summed[:, lanes] + grad_v[:, lanes]
    for b in range(ZN):
        blocks[b, :, 0:CHIP] = summed[:, b * CHIP : (b + 1) * CHIP]
    have(0)
    total = partial(z)
    take(2)
    have(1)
    total = total + partial(ring(-1)) + partial(ring(1))
    take(3)
    take(4)
    have(2)
    total = total + partial(ring(-2)) + partial(ring(2))
    have(3)
    total = total + partial(ring(-3)) + partial(ring(3))
    have(4)
    total = total + partial(ring(4))

    pl.semaphore_wait(here_x, 3)
    for h in range(2):
        part_tiles[h] = total[:, 128 * h : 128 * h + 128]

    def tile(ref, q):
        return ref.at[q // 16, pl.ds(pl.multiple_of(lax.rem(q, 16) * 8, 8), 8), :]

    def spread(src, dst, index):
        def send(q):
            pltpu.make_async_remote_copy(
                src_ref=src(q), dst_ref=dst,
                send_sem=plane_send.at[index], recv_sem=plane_recv.at[index],
                device_id=(r, q), device_id_type=MESH,
            ).start()

        each_of_plane(send)

    def plane_wait(sem):
        pltpu.make_async_copy(
            part_in.at[pl.ds(0, CN - 1)], part_in.at[pl.ds(0, CN - 1)], sem
        ).wait()

    spread(lambda q: tile(part_tiles, q), part_in.at[c], 0)
    part_in[c] = part_tiles[c // 16, pl.ds(pl.multiple_of(lax.rem(c, 16) * 8, 8), 8), :]
    for b in range(ZN):
        blocks_t[b] = jnp.transpose(blocks[b, :, 0:CHIP])
    finish()
    plane_wait(plane_recv.at[0])
    own_tile = part_in[0]
    for q in range(1, CN):
        own_tile = own_tile + part_in[q]
    left_tiles[c // 16, pl.ds(pl.multiple_of(lax.rem(c, 16) * 8, 8), 8), :] = own_tile
    spread(lambda q: tile(left_tiles, c), tile(left_tiles, c), 1)
    plane_wait(plane_recv.at[1])
    left = jnp.concatenate([left_tiles[0], left_tiles[1]], axis=1)

    def give(dist):
        zz = ring(dist)
        return pltpu.make_async_remote_copy(
            src_ref=product.at[at(zz, 1 - core), :], dst_ref=product_in.at[zz],
            send_sem=half_send.at[dist], recv_sem=half_recv.at[dist],
            device_id=sister, device_id_type=MESH,
        )

    def multiply(dist):
        zz = ring(dist)
        product[pl.ds(pl.multiple_of(zz * CHIP, 8), CHIP), :] = dot(blocks_t[zz], left)
        give(dist).start()

    def add_sister(dist):
        zz = ring(dist)
        give(dist).wait_recv()
        product[at(zz, core), :] = product[at(zz, core), :] + product_in[zz]

    def onward(way, dist, s):
        lo, n = SUBS[s]
        return pltpu.make_async_remote_copy(
            src_ref=product.at[at(ring(SIGN[way] * dist), core, lo, n), :],
            dst_ref=passing.at[way, dist - 1, pl.ds(lo, n), :],
            send_sem=rs_send.at[way, dist - 1, s], recv_sem=rs_recv.at[way, dist - 1, s],
            device_id=along(SIGN[way] * (dist - PARENT[dist])), device_id_type=MESH,
        )

    def scatter(dist, some):
        for s in some:
            lo, n = SUBS[s]
            for way in (0, 1):
                rows = at(ring(SIGN[way] * dist), core, lo, n)
                value = product[rows, :]
                for earlier in (3, 4, 2, 1):
                    if PARENT[earlier] == dist and s in pieces(earlier, way):
                        onward(way, earlier, s).wait_recv()
                        value = value + passing[way, earlier - 1, lo : lo + n, :]
                product[rows, :] = value
                if dist > 0:
                    onward(way, dist, s).start()
            if dist == 0:
                gather_piece(s)

    def scatter_finish():
        for dist in range(8):
            give(dist).wait_send()
        for dist in range(1, 5):
            for way in (0, 1):
                for s in pieces(dist, way):
                    onward(way, dist, s).wait_send()

    start2, take2, have2, finish2, over2 = ring_gather(
        right_p, right_p.at[at(z, core), :], ring2_send, ring2_recv, pair2_send, pair2_recv
    )

    def gather_piece(s):
        lo, n = SUBS[s]
        rows = at(z, core, lo, n)
        right_p[rows, :] = product[rows, :]
        start2(s)

    for dist in (4, 3, 5):
        multiply(dist)

    for h in range(2):
        left_t[128 * h : 128 * h + 128, :] = jnp.transpose(left_tiles[h])
    gram_rows = dot(left_t[pl.ds(pl.multiple_of(c * 8, 8), 8), :], left)
    for h in range(2):
        gram_part[h] = gram_rows[:, 128 * h : 128 * h + 128]

    def send_line(q):
        pltpu.make_async_remote_copy(
            src_ref=gram_part.at[lax.rem(q, 2)], dst_ref=gram_in.at[r],
            send_sem=line_send, recv_sem=line_recv,
            device_id=(q, c), device_id_type=MESH,
        ).start()

    each_of_line(send_line)
    gram_in[r] = gram_part[core]

    for dist in (4, 3, 5):
        add_sister(dist)
    for s in range(NS):
        for way in (0, 1):
            if s in pieces(4, way):
                onward(way, 4, s).start()
            onward(way, 3, s).start()
    for dist in (2, 6, 1, 7, 0):
        multiply(dist)
    row = lax.broadcasted_iota(jnp.int32, (RANK, HALF), 0)
    lane = lax.broadcasted_iota(jnp.int32, (RANK, HALF), 1)
    for h in range(2):
        x_ref[h] = jnp.where(row == lane + 128 * h, 1.0, 0.0).astype(F32)
    for dist in (2, 6, 1, 7, 0):
        add_sister(dist)

    def line_wait(sem):
        pltpu.make_async_copy(
            gram_in.at[pl.ds(0, RN - 1)], gram_in.at[pl.ds(0, RN - 1)], sem
        ).wait()

    scatter(2, (0, 1))
    line_wait(line_recv)
    gram_tile = gram_in[0]
    for q in range(1, RN):
        gram_tile = gram_tile + gram_in[q]
    gram_at = pl.ds(pl.multiple_of(c * 8, 8), 8)
    m_ref[core, gram_at, :] = gram_tile
    spread(lambda q: m_ref.at[core, gram_at, :], m_ref.at[core, gram_at, :], 2)
    scatter(2, (2, 3))
    scatter(1, range(NS))
    scatter(0, (0, 1))
    plane_wait(plane_recv.at[2])
    to_sister = pltpu.make_async_remote_copy(
        src_ref=m_ref.at[core], dst_ref=m_ref.at[core],
        send_sem=sister_send, recv_sem=sister_recv,
        device_id=sister, device_id_type=MESH,
    )
    to_sister.start()
    scatter(0, (2, 3))
    over2(0, 0).start()
    plane_wait(plane_send.at[2])
    to_sister.wait()

    units = inverse_factor(m_ref, x_ref)

    def advance(count):
        for _ in range(count):
            next(units, None)

    for before, dists in ((2, (1,)), (6, (2,)), (11, (3, 4))):
        advance(before)
        for s in range(NS):
            for dist in dists:
                take2(dist, (s,))
            advance(2 if dists[0] < 3 else 1)
    for _ in units:
        pass

    inverse = jnp.concatenate([x_ref[0], x_ref[1]], axis=1)

    inverse_t = split3(jnp.transpose(inverse))

    def right_block(zz, own=False):
        rows = pl.ds(pl.multiple_of(zz * CHIP, 16), CHIP)
        value = split3_dot(split3(right_p[rows, :]), inverse_t)
        high, low = split(value)
        right_high[rows, :] = high
        right_low[rows, :] = low
        if own:
            own_right[...] = value
        return jnp.sum((value * value).reshape(CHIP // 8, 8, RANK), axis=0)

    squares = jnp.zeros((8, RANK), F32)
    basis = dot_t(left, inverse)
    for dist in range(5):
        have2(dist)
        if dist == 0:
            squares = squares + right_block(z, own=True)
        elif dist == 4:
            squares = squares + right_block(ring(4))
        else:
            squares = squares + right_block(ring(-dist)) + right_block(ring(dist))
    squares = jnp.sum(squares, axis=0, keepdims=True)
    which = lax.broadcasted_iota(jnp.int32, (8, HALF), 0)
    square_tile = jnp.where(which == 0, squares[:, 0:128], squares[:, 128:256])
    square_part[...] = square_tile
    square_in[c] = square_tile
    spread(lambda q: square_part, square_in.at[c], 3)

    basis_split = split(basis)
    for n in range(0, COLS, 128):
        lanes = slice(n, n + 128)
        right_n = (right_high[lanes, :], right_low[lanes, :])
        out_ref[:, lanes] = summed[:, lanes] - feedback * split_dot_t(basis_split, right_n)
    for index in (0, 1):
        plane_wait(plane_send.at[index])
    line_wait(line_send)
    scatter_finish()
    finish2()

    plane_wait(plane_recv.at[3])
    square_sum = square_in[0]
    for q in range(1, CN):
        square_sum = square_sum + square_in[q]
    norm = jnp.sqrt(square_sum) + epsilon
    norm = jnp.concatenate([norm[0:1, :], norm[1:2, :]], axis=1)
    mine = pl.ds(pl.multiple_of(core * OWN, 8), OWN)
    new_factor_ref[...] = own_right[mine, :] / norm
    multiplier = math.sqrt(ROWS * RN * COLS * CN / RANK)
    basis_ref[...] = basis * (multiplier / norm)
    plane_wait(plane_send.at[3])


def write_kernel(
    momentum_v, factor_v, basis_ref, right_high, right_low, update_ref, out_ref, new_factor_ref,
    update_v, sems,
):
    copies = [pltpu.make_async_copy(factor_v, new_factor_ref, sems.at[0])]
    step = ROWS // LOADS
    for n in range(LOADS):
        rows = pl.ds(n * step, step)
        copies.append(
            pltpu.make_async_copy(momentum_v.at[rows, :], out_ref.at[rows, :], sems.at[1 + n])
        )
    for copy in copies:
        copy.start()
    basis = split(basis_ref[...])
    for i, n in enumerate(range(0, COLS, 128)):
        lanes = slice(n, n + 128)
        update_v[:, lanes] = split_dot_t(basis, (right_high[lanes, :], right_low[lanes, :]))
        copy = pltpu.make_async_copy(
            update_v.at[:, pl.ds(n, 128)], update_ref.at[:, pl.ds(n, 128)], sems.at[1 + LOADS + i]
        )
        copy.start()
        copies.append(copy)
    for copy in copies:
        copy.wait()


def per_device(grad, momentum, factor):
    vmem = pl.BlockSpec(memory_space=pltpu.VMEM)
    hbm = pl.BlockSpec(memory_space=pltpu.HBM)
    dma = pltpu.SemaphoreType.DMA
    out_shape = (
        jax.ShapeDtypeStruct((ROWS, COLS), F32),
        jax.ShapeDtypeStruct((OWN, RANK), F32),
        jax.ShapeDtypeStruct((ROWS, RANK), F32),
        jax.ShapeDtypeStruct((COLS, RANK), BF16),
        jax.ShapeDtypeStruct((COLS, RANK), BF16),
    )
    scratch = [
        pltpu.VMEM((ROWS, COLS), F32),
        pltpu.VMEM((ROWS, COLS), F32),
        pltpu.VMEM((ZN, ROWS, 256), F32),
        pltpu.VMEM((ZN, CHIP, ROWS), F32),
        pltpu.VMEM((COLS, RANK), F32),
        pltpu.VMEM((2, ROWS, HALF), F32),
        pltpu.VMEM((CN, 8, HALF), F32),
        pltpu.VMEM((2, ROWS, HALF), F32),
        pltpu.VMEM((RANK, ROWS), F32),
        pltpu.VMEM((2, 8, HALF), F32),
        pltpu.VMEM((RN, 8, HALF), F32),
        pltpu.VMEM((2, RANK, HALF), F32),
        pltpu.VMEM((2, RANK, HALF), F32),
        pltpu.VMEM((COLS, RANK), F32),
        pltpu.VMEM((ZN, OWN, RANK), F32),
        pltpu.VMEM((2, 4, OWN, RANK), F32),
        pltpu.VMEM((COLS, RANK), F32),
        pltpu.VMEM((CHIP, RANK), F32),
        pltpu.VMEM((8, HALF), F32),
        pltpu.VMEM((CN, 8, HALF), F32),
        dma((2 * LOADS + 1,)),
        dma((2, 4, NS)), dma((2, 4, NS)),
        dma((2, 5)), dma((2, 5)),
        dma((2, 4, NS)), dma((2, 4, NS)),
        dma((8,)), dma((8,)),
        dma((2, 4, NS)), dma((2, 4, NS)),
        dma((2, 5)), dma((2, 5)),
        dma((4,)), dma((4,)),
        dma, dma,
        dma, dma,
        pltpu.SemaphoreType.REGULAR, pltpu.SemaphoreType.REGULAR,
    ]
    sent = pl.pallas_call(
        kernel,
        out_shape=out_shape,
        in_specs=[hbm, hbm, hbm],
        out_specs=(vmem,) * 5,
        scratch_shapes=scratch,
        compiler_params=pltpu.CompilerParams(
            collective_id=0, has_side_effects=True, vmem_limit_bytes=52224 * 1024
        ),
    )(grad, momentum, factor)
    full = jax.ShapeDtypeStruct((ROWS, COLS), F32)
    return pl.pallas_call(
        write_kernel,
        out_shape=(full, full, jax.ShapeDtypeStruct((OWN, RANK), F32)),
        in_specs=[vmem] * 5,
        out_specs=(hbm,) * 3,
        scratch_shapes=[pltpu.VMEM((ROWS, COLS), F32), dma((1 + LOADS + COLS // 128,))],
        compiler_params=pltpu.CompilerParams(vmem_limit_bytes=16 * 1024 * 1024),
    )(*sent)


def solution(mesh):
    return jax.shard_map(
        per_device,
        mesh=mesh,
        in_specs=(P("row", "col"), P("row", "col"), P(("col", "row"), None)),
        out_specs=(P("row", "col"), P("row", "col"), P(("col", "row"), None)),
        check_vma=False,
    )
```
